32 devices in a mesh: mode: 8 (over z, y), mer: 4 (over x, core).
Axes of the slice: x: 2, y: 2, z: 4, core: 2. Of those that a mesh axis runs over, the one named last changes fastest.
Arguments:
- mode_cost: int32 [32], replicated, may hold values from 105 to 420, as said below
- iface_index: int32 [128], replicated, may hold values from 0 to 255, as said below
- basis: float32 [4, 2, 64, 128, 256], P(None, None, 'mode', 'mer'), as said below
- radial: float32 [2, 256, 256], replicated, as said below
- axial: float32 [2, 128, 32], P(None, 'mer'), as said below
- flow_coupling: float32 [4, 128, 256], P(None, 'mer'), may hold values from -8 to 8
- swirl: float32 [128, 256], P('mer'), may hold values from -6 to 6
- shift: float32 [2], replicated, may hold values from 0.2 to 0.8
Outputs:
- new_vector: float32 [2, 64, 128, 256], P(None, 'mode', 'mer')
- coeffs: float32 [2, 4], replicated
- norm: float32 [], replicated
The draws below stay inside these ranges and needn't reach their ends.
Inputs may be any that keep to these rules, and one draw needn't show every extreme that they name: `mode_cost`: every group has 2 to 8 modes and one group has exactly 8; within a group all costs are equal. `iface_index`: distinct and increasing; the first is 0 and the last is 255. `basis`: entries of order one to some tens. `radial`: each matrix has a unit diagonal plus entries of order 1 / sqrt(256). `axial`: each block has a unit diagonal plus entries of order 1 / sqrt(32).
All inputs are finite; a program needn't handle non-finite values.
Results may differ from the reference program's by a relative error of at most 0.000075.
Values sent between devices are 32-bit elements; how exact they have to be, the bound alone decides.
A program may use at most 64 MiB of HBM per device.

```python
import jax
import jax.numpy as jnp
from jax import lax

NR = 256
IFACE = 128
NZ_DEV = 32
MODES_DEV = 4
SLOTS = 8
KRYLOV = 4
QUOTA = 840
MODES = 32
NZ = 128
N_MODE = 8
N_MER = 4


def draw_mode_cost(key, part):
    groups = MODES // MODES_DEV
    pairs = groups // 2
    key_delta = jax.random.fold_in(key, 11)
    key_pick = jax.random.fold_in(key, 12)
    delta = jax.random.randint(key_delta, (pairs,), -2, 3)
    picked = jax.random.randint(key_pick, (), 0, pairs)
    partner = (picked + 1) % pairs
    places = jnp.arange(pairs)
    first = MODES_DEV + delta
    second = MODES_DEV - delta
    first = jnp.where(places == picked, SLOTS, jnp.where(places == partner, 2, first))
    second = jnp.where(places == picked, 2, jnp.where(places == partner, 2 * MODES_DEV - 2, second))
    sizes = jnp.stack([first, second], axis=1).reshape(groups).astype(jnp.int32)
    ends = jnp.cumsum(sizes)
    modes = jnp.arange(MODES)
    group = jnp.sum((modes[:, None] >= ends[None, :]).astype(jnp.int32), axis=1)
    return (QUOTA // sizes[group]).astype(jnp.int32)


def draw_iface_index(key, part):
    inner = jax.random.permutation(jax.random.fold_in(key, 21), NR - 2)[:IFACE - 2] + 1
    ends = jnp.array([0, NR - 1], dtype=jnp.int32)
    return jnp.sort(jnp.concatenate([ends, inner.astype(jnp.int32)]))


def draw_basis(key, part):
    total_slots = MODES // MODES_DEV * SLOTS
    shape = (KRYLOV, 2, total_slots, NZ, NR)
    key_common = jax.random.fold_in(key, 31)
    key_own = jax.random.fold_in(key, 32)
    key_slot = jax.random.fold_in(key, 33)
    key_rad = jax.random.fold_in(key, 34)
    slot_frac = jax.random.uniform(key_slot, (total_slots,), jnp.float32)
    radial_frac = jax.random.uniform(key_rad, (NR,), jnp.float32)
    common = jax.random.truncated_normal(key_common, -4.0, 4.0, shape[1:], jnp.float32)
    own = jax.random.truncated_normal(key_own, -4.0, 4.0, shape, jnp.float32)
    mixed = 0.6 * common[None] + 0.8 * own
    scale = jnp.exp(jnp.log(10.0) * slot_frac)[:, None, None] * jnp.exp(jnp.log(3.0) * radial_frac)[None, None, :]
    return mixed * scale[None, None]


def draw_radial(key, part):
    key = jax.random.fold_in(key, 41)
    rows = jnp.arange(NR)
    identity = (rows[:, None] == rows[None, :]).astype(jnp.float32)
    noise = jax.random.truncated_normal(key, -4.0, 4.0, (2, NR, NR), jnp.float32)
    return identity[None] + 0.5 * noise / jnp.sqrt(float(NR))


def draw_axial(key, part):
    key = jax.random.fold_in(key, 51)
    rows = jnp.arange(NZ) % NZ_DEV
    cols = jnp.arange(NZ_DEV)
    identity = (rows[:, None] == cols[None, :]).astype(jnp.float32)
    noise = jax.random.truncated_normal(key, -4.0, 4.0, (2, NZ, NZ_DEV), jnp.float32)
    return identity[None] + 0.5 * noise / jnp.sqrt(float(NZ_DEV))


def level_of(stream_key, dims, shards, least, high):
    def one(axis_at, shards_of):
        draws = jax.random.uniform(jax.random.fold_in(jax.random.fold_in(stream_key, 6), axis_at), (shards_of,), jnp.float32, least / len(shards), high / len(shards))
        return jnp.repeat(jnp.exp(draws), dims[axis_at] // shards_of).reshape((-1,) + (1,) * (len(dims) - axis_at - 1))

    factor_of = one(*shards[0])
    for cut in shards[1:]:
        factor_of = factor_of * one(*cut)
    return factor_of


def normal_values(key, shape, width, limit, split=(), kind=jnp.bfloat16):
    entries = width * jax.random.normal(key, shape, jnp.float32)
    if split:
        entries = entries * level_of(key, shape, split, -0.22, 0.18)
    return jnp.clip(entries, -limit, limit).astype(kind)


def setup_inputs(seed: int = 0) -> dict:
    key_list = jax.random.split(jax.random.key(seed), 9)
    mode_cost = draw_mode_cost(jax.random.fold_in(key_list[8], 71), 0)
    iface_index = draw_iface_index(jax.random.fold_in(key_list[8], 71), 0)
    basis = draw_basis(jax.random.fold_in(key_list[8], 71), 0)
    radial = draw_radial(jax.random.fold_in(key_list[8], 71), 0)
    axial = draw_axial(jax.random.fold_in(key_list[8], 71), 0)
    flow_coupling = normal_values(key_list[5], (4, NZ, NR), 2.0, 8.0, ((1, 4),), jnp.float32)
    swirl = normal_values(key_list[6], (NZ, NR), 1.0, 6.0, ((0, 4),), jnp.float32)
    shift = jnp.clip(jax.random.uniform(key_list[7], (2,), jnp.float32, 0.2, 0.8), 0.2, 0.8)
    return {"mode_cost": mode_cost, "iface_index": iface_index, "basis": basis, "radial": radial, "axial": axial, "flow_coupling": flow_coupling, "swirl": swirl, "shift": shift}


penalty = 1.0
schur_diag = 2.2
epsilon = 1e-06

def slot_layout(mode_cost):
    prefix = jnp.cumsum(mode_cost) - mode_cost
    owner = (prefix // QUOTA).astype(jnp.int32)
    devices = jnp.arange(N_MODE, dtype=jnp.int32)
    starts = lax.optimization_barrier(jnp.sum((owner[None, :] < devices[:, None]).astype(jnp.int32), axis=1))
    within = jnp.arange(MODES, dtype=jnp.int32) - starts[owner]
    return (owner * SLOTS + within).astype(jnp.int32)

def solve_interface(rhs):
    count = rhs.shape[0]
    places = jnp.arange(count)
    diagonal = jnp.full((count,), schur_diag, rhs.dtype)
    below = jnp.where(places > 0, -1.0, 0.0).astype(rhs.dtype)
    above = jnp.where(places < count - 1, -1.0, 0.0).astype(rhs.dtype)
    return lax.linalg.tridiagonal_solve(below, diagonal, above, rhs)

def reference(mode_cost, iface_index, basis, radial, axial, flow_coupling, swirl, shift):
    highest = lax.Precision.HIGHEST
    slot_of = slot_layout(mode_cost)
    vectors = jnp.take(basis, slot_of, axis=2)
    current = vectors[KRYLOV - 1]
    radial_term = jnp.einsum('cmzr,tr->cmzt', current, radial[0], precision=highest)
    blocked = current.reshape(2, MODES, N_MER, NZ_DEV, NR)
    block_op = axial[0].reshape(N_MER, NZ_DEV, NZ_DEV)
    block_inv = axial[1].reshape(N_MER, NZ_DEV, NZ_DEV)
    axial_term = jnp.einsum('bij,cmbjr->cmbir', block_op, blocked, precision=highest)
    link = jnp.zeros_like(blocked)
    link = link.at[:, :, 1:, 0].add(blocked[:, :, :-1, -1])
    link = link.at[:, :, :-1, -1].add(blocked[:, :, 1:, 0])
    image = radial_term + (axial_term + penalty * link).reshape(2, MODES, NZ, NR)
    padded = jnp.pad(current, ((0, 0), (2, 2), (0, 0), (0, 0)))
    for which, offset in enumerate((-2, -1, 1, 2)):
        image = image + flow_coupling[which] * padded[:, 2 + offset:2 + offset + MODES]
    wave = jnp.arange(MODES).astype(jnp.float32) / MODES
    rotation = wave[:, None, None] * swirl[None]
    image_re = image[0] - rotation * current[1]
    image_im = image[1] + rotation * current[0]
    shifted_re = image_re - (shift[0] * current[0] - shift[1] * current[1])
    shifted_im = image_im - (shift[0] * current[1] + shift[1] * current[0])
    shifted = jnp.stack([shifted_re, shifted_im]).reshape(2, MODES, N_MER, NZ_DEV, NR)
    local = jnp.einsum('bij,cmbjr->cmbir', block_inv, shifted, precision=highest)
    local = jnp.einsum('cmbir,tr->cmbit', local, radial[1], precision=highest)
    jumps = local[:, :, :-1, -1, :] - local[:, :, 1:, 0, :]
    chosen = jnp.take(jumps, iface_index, axis=3)
    rhs = jnp.moveaxis(chosen, 2, 0)
    solved = solve_interface(rhs.reshape(N_MER - 1, -1)).reshape(rhs.shape)
    zero_row = jnp.zeros((1,) + rhs.shape[1:], rhs.dtype)
    padded_g = jnp.moveaxis(jnp.concatenate([zero_row, solved, zero_row], axis=0), 0, 2)
    position = jnp.arange(NZ_DEV).astype(jnp.float32) / (NZ_DEV - 1)
    lower_w = (1.0 - position)[None, None, None, :, None]
    upper_w = position[None, None, None, :, None]
    correction = lower_w * padded_g[:, :, :-1, None, :] - upper_w * padded_g[:, :, 1:, None, :]
    local = local.at[..., iface_index].add(correction)
    result = local.reshape(2, MODES, NZ, NR)
    dof = float(MODES * NZ * NR)
    proj_re = lax.optimization_barrier(jnp.sum(vectors * result[None], axis=(1, 2, 3, 4))) / dof
    proj_im = lax.optimization_barrier(jnp.sum(vectors[:, 0] * result[None, 1] - vectors[:, 1] * result[None, 0], axis=(1, 2, 3))) / dof
    rest_re = result[0] - lax.optimization_barrier(jnp.sum(proj_re[:, None, None, None] * vectors[:, 0] - proj_im[:, None, None, None] * vectors[:, 1], axis=0))
    rest_im = result[1] - lax.optimization_barrier(jnp.sum(proj_re[:, None, None, None] * vectors[:, 1] + proj_im[:, None, None, None] * vectors[:, 0], axis=0))
    total = (jnp.sum(rest_re * rest_re) + jnp.sum(rest_im * rest_im)) / dof
    norm = jnp.sqrt(total + epsilon)
    fresh = jnp.stack([rest_re, rest_im]) / norm
    new_vector = jnp.zeros((2, N_MODE * SLOTS, NZ, NR), fresh.dtype).at[:, slot_of].set(fresh)
    return (new_vector, jnp.stack([proj_re, proj_im]), norm)
```

```python
import functools

import jax
import jax.numpy as jnp
import numpy as np
from jax import lax
from jax.experimental import pallas as pl
from jax.experimental.pallas import tpu as pltpu
from jax.sharding import PartitionSpec as P

QUOTA = 840

penalty = 1.0
schur_diag = 2.2
epsilon = 1e-06

F32 = jnp.float32
BF16 = jnp.bfloat16


def split(x):
    hi = x.astype(BF16)
    return hi, (x - hi.astype(F32)).astype(BF16)


def mm(a, b):
    return lax.dot_general(a, b, (((1,), (0,)), ((), ())), preferred_element_type=F32)


def mmt(a, b):
    return lax.dot_general(a, b, (((1,), (1,)), ((), ())), preferred_element_type=F32)


def kernel(
    n_mode, n_mer, modes,
    cost, shift, iface, basis, radial, axial, flow, swirl,
    out, coef, norm,
    cur, ext, bas, rad, axl, flw, swl, ifc,
    stage, low, up, first, last, mlo, mhi,
    rh, rl, dh, dl, img, loc, trs, part, red_mer, red_mode,
    local_sem, halo_send, halo_recv, tr_send, tr_recv, ra_send, ra_recv, rb_send, rb_recv,
):
    krylov, _, slots, points, width = basis.shape
    rows = slots * points
    tiles = points // 8
    mode = lax.axis_index("mode")
    mer = lax.axis_index("mer")

    def at_mode(i):
        return {"mode": i}

    def at_mer(i):
        return {"mer": i}

    mesh_id = pl.DeviceIdType.MESH
    barrier = pltpu.get_barrier_semaphore()
    for i in range(1, n_mer):
        pl.semaphore_signal(barrier, inc=1, device_id=at_mer(lax.rem(mer + i, n_mer)), device_id_type=mesh_id)
    for i in range(1, n_mode):
        pl.semaphore_signal(barrier, inc=1, device_id=at_mode(lax.rem(mode + i, n_mode)), device_id_type=mesh_id)

    loads = [
        pltpu.make_async_copy(basis.at[krylov - 1], cur, local_sem.at[0]),
        pltpu.make_async_copy(axial, axl, local_sem.at[1]),
        pltpu.make_async_copy(iface, ifc, local_sem.at[2]),
        pltpu.make_async_copy(radial, rad, local_sem.at[3]),
        pltpu.make_async_copy(basis.at[krylov - 1], ext.at[:, 2 : 2 + slots], local_sem.at[4]),
        pltpu.make_async_copy(basis.at[0 : krylov - 1], bas, local_sem.at[5]),
        pltpu.make_async_copy(flow, flw, local_sem.at[6]),
        pltpu.make_async_copy(swirl, swl, local_sem.at[7]),
    ]
    for load in loads:
        load.start()

    least = mode * QUOTA

    def layout(k, carry):
        prefix, start, upto = carry
        start = start + (prefix < least).astype(jnp.int32)
        upto = upto + (prefix < least + QUOTA).astype(jnp.int32)
        return prefix + cost[k], start, upto

    zero = jnp.int32(0)
    _, start, upto = lax.fori_loop(0, modes, layout, (zero, zero, zero), unroll=8)
    count = upto - start
    ending = jnp.clip(count, 2, slots) - 2

    loads[0].wait()
    for c in range(2):
        for i in range(2):
            stage[c, i] = cur[c, ending + i]
        for s in range(slots):
            first[c, s : s + 1, :] = cur[c, s, 0:1, :]
            last[c, s : s + 1, :] = cur[c, s, points - 1 : points, :]

    def halo(which, src, dst, device):
        return pltpu.make_async_remote_copy(
            src_ref=src, dst_ref=dst, send_sem=halo_send.at[which], recv_sem=halo_recv.at[which],
            device_id=device, device_id_type=mesh_id,
        )

    to_next = halo(0, stage, low, at_mode(lax.rem(mode + 1, n_mode)))
    to_prev = halo(1, cur.at[:, 0:2], up, at_mode(lax.rem(mode + n_mode - 1, n_mode)))
    to_right = halo(2, last, mlo, at_mer(lax.rem(mer + 1, n_mer)))
    to_left = halo(3, first, mhi, at_mer(lax.rem(mer + n_mer - 1, n_mer)))
    has_next, has_prev = mode < n_mode - 1, mode > 0
    has_right, has_left = mer < n_mer - 1, mer > 0
    pl.semaphore_wait(barrier, n_mer - 1 + n_mode - 1)
    for there, copy in ((has_next, to_next), (has_prev, to_prev), (has_right, to_right), (has_left, to_left)):

        @pl.when(there)
        def _(copy=copy):
            copy.start()

    loads[1].wait()
    col = lax.broadcasted_iota(jnp.int32, (points, width), 1)
    row = lax.broadcasted_iota(jnp.int32, (points, width), 0)
    spread = col == row
    for s in range(1, slots):
        spread = jnp.logical_or(spread, col == row + s * points)
    spread = jnp.where(spread, 1.0, 0.0).astype(BF16)
    col8 = lax.broadcasted_iota(jnp.int32, (slots, width), 1)
    base8 = lax.broadcasted_iota(jnp.int32, (slots, width), 0) * points
    mine8 = jnp.logical_and(col8 >= base8, col8 < base8 + points)
    for k in range(2):
        for part_of, to in zip(split(axl[k]), (dh, dl)):
            wide = mm(part_of, spread)
            for s in range(slots):
                block = jnp.logical_and(col >= s * points, col < (s + 1) * points)
                to[k, s * points : (s + 1) * points, :] = jnp.where(block, wide, 0.0).astype(BF16)
            if k == 1:
                top = jnp.where(mine8, jnp.broadcast_to(wide[points - 1 : points], (slots, width)), 0.0)
                bottom = jnp.where(mine8, jnp.broadcast_to(wide[0:1], (slots, width)), 0.0)
                to[k, rows : rows + 2 * slots, :] = jnp.concatenate([top, bottom], axis=0).astype(BF16)

    loads[2].wait()
    places = lax.broadcasted_iota(jnp.int32, (width, ifc.shape[1]), 0)
    chosen = jnp.where(places == ifc[...], 1.0, 0.0).astype(BF16)
    mask = mmt(jnp.ones((8, ifc.shape[1]), BF16), chosen)

    loads[3].wait()
    for k in range(2):
        rh[k], rl[k] = split(rad[k])
    for c in range(2):
        xh, xl = split(cur[c].reshape(rows, width))
        total = mmt(xh, rh[0]) + mmt(xl, rh[0]) + mmt(xh, rl[0])
        total = total + mm(dh[0, 0:rows], xh) + mm(dl[0, 0:rows], xh) + mm(dh[0, 0:rows], xl)
        img[c] = total.reshape(slots, points, width)

    loads[5].wait()
    pairs = [(i, j) for i in range(krylov) for j in range(i, krylov)]
    cross = [(i, j) for i in range(krylov) for j in range(i + 1, krylov)]

    def fold(x):
        half = x[:, 0:128]
        for at in range(128, width, 128):
            half = half + x[:, at : at + 128]
        return jnp.sum(half, axis=0, keepdims=True)

    def gram(s, carry):
        carry = list(carry)
        live = s < count
        for t in range(tiles):
            z = pl.ds(t * 8, 8)
            q = [[bas[j, c, s, z, :] for c in range(2)] for j in range(krylov - 1)]
            q.append([cur[c, s, z, :] for c in range(2)])
            q = [[jnp.where(live, x, 0.0) for x in both] for both in q]
            for n, (i, j) in enumerate(pairs):
                carry[n] = carry[n] + (q[i][0] * q[j][0] + q[i][1] * q[j][1])
            for n, (i, j) in enumerate(cross):
                n += len(pairs)
                carry[n] = carry[n] + (q[i][0] * q[j][1] - q[i][1] * q[j][0])
        return tuple(carry)

    empty = jnp.zeros((8, width), F32)
    grams = lax.fori_loop(0, slots, gram, (empty,) * (len(pairs) + len(cross)))
    n_inner = 2 * krylov + 1
    part[...] = jnp.zeros(part.shape, F32)
    for n, x in enumerate(grams):
        part[n_inner + n : n_inner + n + 1, :] = fold(x)

    loads[4].wait()
    loads[6].wait()
    loads[7].wait()

    @pl.when(has_prev)
    def _():
        to_next.wait_recv()
        ext[:, 0:2] = low[...]

    @pl.when(jnp.logical_not(has_prev))
    def _():
        ext[:, 0:2] = jnp.zeros(low.shape, F32)

    @pl.when(has_next)
    def _():
        to_prev.wait_recv()
        for i in range(2):
            ext[:, 2 + slots + i] = jnp.where(upto + i < modes, up[:, i], 0.0)

    @pl.when(jnp.logical_not(has_next))
    def _():
        ext[:, 2 + slots : 4 + slots] = jnp.zeros(up.shape, F32)

    @pl.when(has_left)
    def _():
        to_right.wait_recv()

    @pl.when(jnp.logical_not(has_left))
    def _():
        mlo[...] = jnp.zeros(mlo.shape, F32)

    @pl.when(has_right)
    def _():
        to_left.wait_recv()

    @pl.when(jnp.logical_not(has_right))
    def _():
        mhi[...] = jnp.zeros(mhi.shape, F32)

    sig_re, sig_im = shift[0], shift[1]
    sub8 = lax.broadcasted_iota(jnp.int32, (8, width), 0)
    for s in range(slots):
        wave = (start + s).astype(F32) / modes
        at = []
        for d in (-2, -1, 1, 2):
            over = s + d - count
            at.append(jnp.where(over < 0, 2 + s + d, 2 + slots + jnp.minimum(over, 1)))
        for t in range(tiles):
            z = slice(t * 8, (t + 1) * 8)
            spin = sig_im - wave * swl[z, :]
            x = (cur[0, s, z, :], cur[1, s, z, :])
            coupling = [flw[i, z, :] for i in range(4)]
            for c in range(2):
                acc = img[c, s, z, :]
                for i in range(4):
                    acc = acc + coupling[i] * ext[c, at[i], z, :]
                turn = spin * x[1] if c == 0 else -(spin * x[0])
                acc = acc - sig_re * x[c] + turn
                if t == 0:
                    acc = acc + jnp.where(sub8 == 0, penalty * mlo[c, s : s + 1, :], 0.0)
                if t == tiles - 1:
                    acc = acc + jnp.where(sub8 == 7, penalty * mhi[c, s : s + 1, :], 0.0)
                img[c, s, z, :] = acc

    inner = []
    for c in range(2):
        xh, xl = split(img[c].reshape(rows, width))
        y = mm(dh[1], xh) + mm(dl[1], xh) + mm(dh[1], xl)
        ends = split(y[rows : rows + 2 * slots])
        both = mmt(ends[0], rh[1]) + mmt(ends[1], rh[1]) + mmt(ends[0], rl[1])
        trs[mer, 0, c] = both[0:slots]
        trs[mer, 1, c] = both[slots : 2 * slots]
        inner.append(y[0:rows])

    def trace(i, slot, to):
        return pltpu.make_async_remote_copy(
            src_ref=trs.at[slot], dst_ref=trs.at[slot], send_sem=tr_send.at[i], recv_sem=tr_recv.at[i],
            device_id=at_mer(to), device_id_type=mesh_id,
        )

    for i in range(1, n_mer):
        trace(i, mer, lax.rem(mer + i, n_mer)).start()
    for c in range(2):
        yh, yl = split(inner[c])
        loc[c] = (mmt(yh, rh[1]) + mmt(yl, rh[1]) + mmt(yh, rl[1])).reshape(slots, points, width)
    for i in range(1, n_mer):
        trace(i, lax.rem(mer + n_mer - i, n_mer), mer).wait_recv()

    count_j = n_mer - 1
    inverse = np.linalg.inv(schur_diag * np.eye(count_j) - np.eye(count_j, k=1) - np.eye(count_j, k=-1))
    inverse = np.pad(inverse, ((1, 1), (0, 0)))
    jumps = [[trs[j, 0, c] - trs[j + 1, 1, c] for c in range(2)] for j in range(count_j)]

    def weight(side, j):
        value = jnp.float32(0.0)
        for b in range(n_mer):
            value = jnp.where(mer == b, jnp.float32(inverse[b + side, j]), value)
        return value

    sides = []
    for side in range(2):
        weights = [weight(side, j) for j in range(count_j)]
        sides.append([mask * sum(w * jump[c] for w, jump in zip(weights, jumps)) for c in range(2)])

    accs = [empty] * n_inner
    height = lax.broadcasted_iota(jnp.int32, (8, width), 0)
    for s in range(slots):
        live = s < count
        for t in range(tiles):
            z = slice(t * 8, (t + 1) * 8)
            position = (height + t * 8).astype(F32) / (points - 1)
            w = []
            for c in range(2):
                x = loc[c, s, z, :] + (1.0 - position) * sides[0][c][s : s + 1] - position * sides[1][c][s : s + 1]
                x = jnp.where(live, x, 0.0)
                loc[c, s, z, :] = x
                w.append(x)
            for j in range(krylov):
                src = cur if j == krylov - 1 else bas.at[j]
                re, im = src[0, s, z, :], src[1, s, z, :]
                accs[j] = accs[j] + (re * w[0] + im * w[1])
                accs[krylov + j] = accs[krylov + j] + (re * w[1] - im * w[0])
            accs[2 * krylov] = accs[2 * krylov] + (w[0] * w[0] + w[1] * w[1])
    for n, x in enumerate(accs):
        part[n : n + 1, :] = fold(x)

    def share(buffer, sends, recvs, i, slot, device):
        return pltpu.make_async_remote_copy(
            src_ref=buffer.at[slot], dst_ref=buffer.at[slot], send_sem=sends.at[i], recv_sem=recvs.at[i],
            device_id=device, device_id_type=mesh_id,
        )

    red_mer[mer] = part[...]
    for i in range(1, n_mer):
        share(red_mer, ra_send, ra_recv, i, mer, at_mer(lax.rem(mer + i, n_mer))).start()
    for i in range(1, n_mer):
        share(red_mer, ra_send, ra_recv, i, lax.rem(mer + n_mer - i, n_mer), at_mer(mer)).wait_recv()
    total = red_mer[0]
    for i in range(1, n_mer):
        total = total + red_mer[i]
    red_mode[mode] = total
    for i in range(1, n_mode):
        share(red_mode, rb_send, rb_recv, i, mode, at_mode(lax.rem(mode + i, n_mode))).start()
    for i in range(1, n_mode):
        share(red_mode, rb_send, rb_recv, i, lax.rem(mode + n_mode - i, n_mode), at_mode(mode)).wait_recv()
    total = red_mode[0]
    for i in range(1, n_mode):
        total = total + red_mode[i]
    dof = float(modes * points * n_mer * width)
    total = jnp.sum(total, axis=1, keepdims=True) / dof
    one = [total[n : n + 1, :] for n in range(n_inner + len(pairs) + len(cross))]
    c_re, c_im = one[0:krylov], one[krylov : 2 * krylov]
    square = one[2 * krylov]
    for j in range(krylov):
        square = square - 2.0 * (c_re[j] * c_re[j] + c_im[j] * c_im[j])
    for n, (i, j) in enumerate(pairs):
        both = c_re[i] * c_re[j] + c_im[i] * c_im[j]
        square = square + (1.0 if i == j else 2.0) * both * one[n_inner + n]
    for n, (i, j) in enumerate(cross):
        both = c_re[i] * c_im[j] - c_im[i] * c_re[j]
        square = square - 2.0 * both * one[n_inner + len(pairs) + n]
    size = jnp.sqrt(jnp.maximum(square, 0.0) + epsilon)
    norm[...] = size
    lane = lax.broadcasted_iota(jnp.int32, coef.shape, 1)
    side = lax.broadcasted_iota(jnp.int32, coef.shape, 0)
    table = jnp.zeros(coef.shape, F32)
    for j in range(krylov):
        table = jnp.where(lane == j, jnp.where(side == 0, c_re[j], c_im[j]), table)
    coef[...] = table

    scale = 1.0 / size
    scaled_re = [jnp.broadcast_to(x * scale, (8, width)) for x in c_re]
    scaled_im = [jnp.broadcast_to(x * scale, (8, width)) for x in c_im]
    scale = jnp.broadcast_to(scale, (8, width))
    for s in range(slots):
        live = s < count
        for t in range(tiles):
            z = slice(t * 8, (t + 1) * 8)
            new_re = loc[0, s, z, :] * scale
            new_im = loc[1, s, z, :] * scale
            for j in range(krylov):
                src = cur if j == krylov - 1 else bas.at[j]
                re, im = src[0, s, z, :], src[1, s, z, :]
                new_re = new_re - (scaled_re[j] * re - scaled_im[j] * im)
                new_im = new_im - (scaled_re[j] * im + scaled_im[j] * re)
            out[0, s, z, :] = jnp.where(live, new_re, 0.0)
            out[1, s, z, :] = jnp.where(live, new_im, 0.0)

    for there, copy in ((has_next, to_next), (has_prev, to_prev), (has_right, to_right), (has_left, to_left)):

        @pl.when(there)
        def _(copy=copy):
            copy.wait_send()

    for i in range(1, n_mer):
        trace(i, mer, lax.rem(mer + i, n_mer)).wait_send()
        share(red_mer, ra_send, ra_recv, i, mer, at_mer(lax.rem(mer + i, n_mer))).wait_send()
    for i in range(1, n_mode):
        share(red_mode, rb_send, rb_recv, i, mode, at_mode(lax.rem(mode + i, n_mode))).wait_send()


def body(n_mode, n_mer, mode_cost, iface_index, basis, radial, axial, flow_coupling, swirl, shift):
    krylov, _, slots, points, width = basis.shape
    modes = mode_cost.shape[0]
    rows = slots * points
    sums = 2 * krylov + 1 + krylov * krylov
    sums = (sums + 7) // 8 * 8
    field = (2, slots, points, width)
    pair = (2, 2, points, width)
    ends = (2, slots, width)
    smem = pl.BlockSpec(memory_space=pltpu.SMEM)
    hbm = pl.BlockSpec(memory_space=pl.ANY)
    vmem = pl.BlockSpec(memory_space=pltpu.VMEM)
    dma = pltpu.SemaphoreType.DMA
    new_vector, coeffs, norm = pl.pallas_call(
        functools.partial(kernel, n_mode, n_mer, modes),
        out_shape=[
            jax.ShapeDtypeStruct(field, F32),
            jax.ShapeDtypeStruct((2, krylov), F32),
            jax.ShapeDtypeStruct((1, 1), F32),
        ],
        in_specs=[smem, smem] + [hbm] * 6,
        out_specs=[vmem] * 3,
        scratch_shapes=[
            pltpu.VMEM(field, F32),
            pltpu.VMEM((2, slots + 4, points, width), F32),
            pltpu.VMEM((krylov - 1,) + field, F32),
            pltpu.VMEM(radial.shape, F32),
            pltpu.VMEM(axial.shape, F32),
            pltpu.VMEM(flow_coupling.shape, F32),
            pltpu.VMEM(swirl.shape, F32),
            pltpu.VMEM((1, iface_index.shape[0]), jnp.int32),
            pltpu.VMEM(pair, F32),
            pltpu.VMEM(pair, F32),
            pltpu.VMEM(pair, F32),
            pltpu.VMEM(ends, F32),
            pltpu.VMEM(ends, F32),
            pltpu.VMEM(ends, F32),
            pltpu.VMEM(ends, F32),
            pltpu.VMEM(radial.shape, BF16),
            pltpu.VMEM(radial.shape, BF16),
            pltpu.VMEM((2, rows + 2 * slots, rows), BF16),
            pltpu.VMEM((2, rows + 2 * slots, rows), BF16),
            pltpu.VMEM(field, F32),
            pltpu.VMEM(field, F32),
            pltpu.VMEM((n_mer, 2) + ends, F32),
            pltpu.VMEM((sums, 128), F32),
            pltpu.VMEM((n_mer, sums, 128), F32),
            pltpu.VMEM((n_mode, sums, 128), F32),
            dma((8,)),
            dma((4,)),
            dma((4,)),
            dma((n_mer,)),
            dma((n_mer,)),
            dma((n_mer,)),
            dma((n_mer,)),
            dma((n_mode,)),
            dma((n_mode,)),
        ],
        compiler_params=pltpu.CompilerParams(
            collective_id=0, has_side_effects=True, vmem_limit_bytes=60 * 1024 * 1024
        ),
    )(mode_cost, shift, iface_index[None, :], basis, radial, axial, flow_coupling, swirl)
    return new_vector, coeffs, norm.reshape(())


def solution(mesh):
    in_specs = (
        P(),
        P(),
        P(None, None, "mode", "mer", None),
        P(),
        P(None, "mer", None),
        P(None, "mer", None),
        P("mer", None),
        P(),
    )
    out_specs = (P(None, "mode", "mer", None), P(), P())
    program = functools.partial(body, mesh.shape["mode"], mesh.shape["mer"])
    return jax.shard_map(program, mesh=mesh, in_specs=in_specs, out_specs=out_specs, check_vma=False)
```

```python
import functools

import jax
import jax.numpy as jnp
import numpy as np
from jax import lax
from jax.experimental import pallas as pl
from jax.experimental.pallas import tpu as pltpu
from jax.sharding import PartitionSpec as P

QUOTA = 840

penalty = 1.0
schur_diag = 2.2
epsilon = 1e-06

F32 = jnp.float32
BF16 = jnp.bfloat16


def split(x):
    hi = x.astype(BF16)
    return hi, (x - hi.astype(F32)).astype(BF16)


def mm(a, b):
    return lax.dot_general(a, b, (((1,), (0,)), ((), ())), preferred_element_type=F32)


def mmt(a, b):
    return lax.dot_general(a, b, (((1,), (1,)), ((), ())), preferred_element_type=F32)


def diagonal(size):
    row = lax.broadcasted_iota(jnp.int32, (size, 128), 0)
    return row == lax.broadcasted_iota(jnp.int32, (size, 128), 1)


def to_row(column):
    return jnp.sum(jnp.where(diagonal(column.shape[0]), column, 0.0), axis=0, keepdims=True)


def to_column(row, size):
    return jnp.sum(jnp.where(diagonal(size), row, 0.0), axis=1, keepdims=True)


def finish(dof, basis, w_in, stats, out, coef, norm, bas, w, fresh, in_sem, w_sem, out_sem):
    krylov, _, slots, points, width = basis.shape
    tiles = points // 8
    pairs = [(i, j) for i in range(krylov) for j in range(i, krylov)]
    cross = [(i, j) for i in range(krylov) for j in range(i + 1, krylov)]
    n_inner = 2 * krylov + 1
    sums = n_inner + len(pairs) + len(cross)
    half = slots // 2
    ins, outs = [], []
    for n in range(2):
        at = pl.ds(n * half, half)
        ins.append(pltpu.make_async_copy(basis.at[:, :, at], bas.at[:, :, at], in_sem.at[n]))
        ins.append(pltpu.make_async_copy(w_in.at[:, at], w.at[:, at], w_sem.at[n]))
        outs.append(pltpu.make_async_copy(fresh.at[:, at], out.at[:, at], out_sem.at[n]))
    for copy in ins:
        copy.start()
    count = stats[:, 127:128]
    total = to_column(stats[...], (sums + 7) // 8 * 8) / dof
    one = [total[n : n + 1, :] for n in range(sums)]
    c_re, c_im = one[0:krylov], one[krylov : 2 * krylov]
    square = one[2 * krylov]
    for j in range(krylov):
        square = square - 2.0 * (c_re[j] * c_re[j] + c_im[j] * c_im[j])
    for n, (i, j) in enumerate(pairs):
        both = c_re[i] * c_re[j] + c_im[i] * c_im[j]
        square = square + (1.0 if i == j else 2.0) * both * one[n_inner + n]
    for n, (i, j) in enumerate(cross):
        both = c_re[i] * c_im[j] - c_im[i] * c_re[j]
        square = square - 2.0 * both * one[n_inner + len(pairs) + n]
    size = jnp.sqrt(jnp.maximum(square, 0.0) + epsilon)
    norm[...] = size
    lane = lax.broadcasted_iota(jnp.int32, coef.shape, 1)
    side = lax.broadcasted_iota(jnp.int32, coef.shape, 0)
    table = jnp.zeros(coef.shape, F32)
    for j in range(krylov):
        table = jnp.where(lane == j, jnp.where(side == 0, c_re[j], c_im[j]), table)
    coef[...] = table

    scale = 1.0 / size
    scaled_re = [jnp.broadcast_to(x * scale, (8, width)) for x in c_re]
    scaled_im = [jnp.broadcast_to(x * scale, (8, width)) for x in c_im]
    scale = jnp.broadcast_to(scale, (8, width))
    live_to = jnp.broadcast_to(count, (8, width))
    for s in range(slots):
        if s % half == 0:
            ins[s // half * 2].wait()
            ins[s // half * 2 + 1].wait()
        live = live_to > s
        for t in range(tiles):
            z = slice(t * 8, (t + 1) * 8)
            new_re = w[0, s, z, :] * scale
            new_im = w[1, s, z, :] * scale
            for j in range(krylov):
                re, im = bas[j, 0, s, z, :], bas[j, 1, s, z, :]
                new_re = new_re - (scaled_re[j] * re - scaled_im[j] * im)
                new_im = new_im - (scaled_re[j] * im + scaled_im[j] * re)
            fresh[0, s, z, :] = jnp.where(live, new_re, 0.0)
            fresh[1, s, z, :] = jnp.where(live, new_im, 0.0)
        if s % half == half - 1:
            outs[s // half].start()
    for copy in outs:
        copy.wait()


def kernel(
    n_mode, n_mer, modes,
    cost, shift, iface, basis, radial, axial, flow, swirl,
    w_out, stats,
    cur, bas, rad, axl, flw, swl, ifc,
    stage, low, up, first, last, mlo, mhi,
    rh, rl, dh, dl, img, loc, trs, part, red_mer, red_mode,
    local_sem, w_sem, halo_send, halo_recv, tr_send, tr_recv, ra_send, ra_recv, rb_send, rb_recv,
):
    krylov, _, slots, points, width = basis.shape
    rows = slots * points
    tiles = points // 8
    mode = lax.axis_index("mode")
    mer = lax.axis_index("mer")

    def at_mode(i):
        return {"mode": i}

    def at_mer(i):
        return {"mer": i}

    mesh_id = pl.DeviceIdType.MESH
    barrier = pltpu.get_barrier_semaphore()
    for i in range(1, n_mer):
        pl.semaphore_signal(barrier, inc=1, device_id=at_mer(lax.rem(mer + i, n_mer)), device_id_type=mesh_id)
    for i in range(1, n_mode):
        pl.semaphore_signal(barrier, inc=1, device_id=at_mode(lax.rem(mode + i, n_mode)), device_id_type=mesh_id)

    loads = [
        pltpu.make_async_copy(basis.at[krylov - 1], cur, local_sem.at[0]),
        pltpu.make_async_copy(axial, axl, local_sem.at[1]),
        pltpu.make_async_copy(iface, ifc, local_sem.at[2]),
        pltpu.make_async_copy(radial, rad, local_sem.at[3]),
        pltpu.make_async_copy(flow, flw, local_sem.at[4]),
        pltpu.make_async_copy(swirl, swl, local_sem.at[5]),
        pltpu.make_async_copy(basis.at[0 : krylov - 1], bas, local_sem.at[6]),
    ]
    for load in loads:
        load.start()

    least = mode * QUOTA

    def layout(k, carry):
        prefix, start, upto = carry
        start = start + (prefix < least).astype(jnp.int32)
        upto = upto + (prefix < least + QUOTA).astype(jnp.int32)
        return prefix + cost[k], start, upto

    zero = jnp.int32(0)
    _, start, upto = lax.fori_loop(0, modes, layout, (zero, zero, zero), unroll=8)
    count = upto - start
    ending = jnp.clip(count, 2, slots) - 2

    loads[0].wait()
    for c in range(2):
        for i in range(2):
            stage[c, i] = cur[c, ending + i]
        for s in range(slots):
            first[c, s : s + 1, :] = cur[c, s, 0:1, :]
            last[c, s : s + 1, :] = cur[c, s, points - 1 : points, :]

    def halo(which, src, dst, device):
        return pltpu.make_async_remote_copy(
            src_ref=src, dst_ref=dst, send_sem=halo_send.at[which], recv_sem=halo_recv.at[which],
            device_id=device, device_id_type=mesh_id,
        )

    to_next = halo(0, stage, low, at_mode(lax.rem(mode + 1, n_mode)))
    to_prev = halo(1, cur.at[:, 0:2], up, at_mode(lax.rem(mode + n_mode - 1, n_mode)))
    to_right = halo(2, last, mlo, at_mer(lax.rem(mer + 1, n_mer)))
    to_left = halo(3, first, mhi, at_mer(lax.rem(mer + n_mer - 1, n_mer)))
    has_next, has_prev = mode < n_mode - 1, mode > 0
    has_right, has_left = mer < n_mer - 1, mer > 0
    pl.semaphore_wait(barrier, n_mer - 1 + n_mode - 1)
    for there, copy in ((has_next, to_next), (has_prev, to_prev), (has_right, to_right), (has_left, to_left)):

        @pl.when(there)
        def _(copy=copy):
            copy.start()

    loads[1].wait()
    col = lax.broadcasted_iota(jnp.int32, (points, width), 1)
    row = lax.broadcasted_iota(jnp.int32, (points, width), 0)
    spread = col == row
    for s in range(1, slots):
        spread = jnp.logical_or(spread, col == row + s * points)
    spread = jnp.where(spread, 1.0, 0.0).astype(BF16)
    col8 = lax.broadcasted_iota(jnp.int32, (slots, width), 1)
    base8 = lax.broadcasted_iota(jnp.int32, (slots, width), 0) * points
    mine8 = jnp.logical_and(col8 >= base8, col8 < base8 + points)
    for k in range(2):
        for part_of, to in zip(split(axl[k]), (dh, dl)):
            wide = mm(part_of, spread)
            for s in range(slots):
                block = jnp.logical_and(col >= s * points, col < (s + 1) * points)
                to[k, s * points : (s + 1) * points, :] = jnp.where(block, wide, 0.0).astype(BF16)
            if k == 1:
                top = jnp.where(mine8, jnp.broadcast_to(wide[points - 1 : points], (slots, width)), 0.0)
                bottom = jnp.where(mine8, jnp.broadcast_to(wide[0:1], (slots, width)), 0.0)
                to[k, rows : rows + 2 * slots, :] = jnp.concatenate([top, bottom], axis=0).astype(BF16)

    loads[2].wait()
    places = lax.broadcasted_iota(jnp.int32, (width, ifc.shape[1]), 0)
    chosen = jnp.where(places == ifc[...], 1.0, 0.0).astype(BF16)
    mask = mmt(jnp.ones((8, ifc.shape[1]), BF16), chosen)

    loads[3].wait()
    for k in range(2):
        rh[k], rl[k] = split(rad[k])
    for c in range(2):
        xh, xl = split(cur[c].reshape(rows, width))
        total = mmt(xh, rh[0]) + mmt(xl, rh[0]) + mmt(xh, rl[0])
        total = total + mm(dh[0, 0:rows], xh) + mm(dl[0, 0:rows], xh) + mm(dh[0, 0:rows], xl)
        img[c] = total.reshape(slots, points, width)

    loads[4].wait()
    loads[5].wait()

    @pl.when(has_left)
    def _():
        to_right.wait_recv()

    @pl.when(jnp.logical_not(has_left))
    def _():
        mlo[...] = jnp.zeros(mlo.shape, F32)

    @pl.when(has_right)
    def _():
        to_left.wait_recv()

    @pl.when(jnp.logical_not(has_right))
    def _():
        mhi[...] = jnp.zeros(mhi.shape, F32)

    sig_re, sig_im = shift[0], shift[1]
    sub8 = lax.broadcasted_iota(jnp.int32, (8, width), 0)
    offsets = (-2, -1, 1, 2)
    for s in range(slots):
        wave = (start + s).astype(F32) / modes
        for t in range(tiles):
            z = slice(t * 8, (t + 1) * 8)
            spin = sig_im - wave * swl[z, :]
            x = (cur[0, s, z, :], cur[1, s, z, :])
            for c in range(2):
                acc = img[c, s, z, :]
                for i, d in enumerate(offsets):
                    if 0 <= s + d < slots:
                        other = cur[c, s + d, z, :]
                        if d > 0:
                            other = jnp.where(s + d < count, other, 0.0)
                        acc = acc + flw[i, z, :] * other
                turn = spin * x[1] if c == 0 else -(spin * x[0])
                acc = acc - sig_re * x[c] + turn
                if t == 0:
                    acc = acc + jnp.where(sub8 == 0, penalty * mlo[c, s : s + 1, :], 0.0)
                if t == tiles - 1:
                    acc = acc + jnp.where(sub8 == 7, penalty * mhi[c, s : s + 1, :], 0.0)
                img[c, s, z, :] = acc

    loads[6].wait()
    pairs = [(i, j) for i in range(krylov) for j in range(i, krylov)]
    cross = [(i, j) for i in range(krylov) for j in range(i + 1, krylov)]

    def fold(x):
        half = x[:, 0:128]
        for at in range(128, width, 128):
            half = half + x[:, at : at + 128]
        return jnp.sum(half, axis=0, keepdims=True)

    def gram(s, carry):
        carry = list(carry)
        live = s < count
        for t in range(tiles):
            z = pl.ds(t * 8, 8)
            q = [[bas[j, c, s, z, :] for c in range(2)] for j in range(krylov - 1)]
            q.append([cur[c, s, z, :] for c in range(2)])
            q = [[jnp.where(live, x, 0.0) for x in both] for both in q]
            for n, (i, j) in enumerate(pairs):
                carry[n] = carry[n] + (q[i][0] * q[j][0] + q[i][1] * q[j][1])
            for n, (i, j) in enumerate(cross):
                n += len(pairs)
                carry[n] = carry[n] + (q[i][0] * q[j][1] - q[i][1] * q[j][0])
        return tuple(carry)

    empty = jnp.zeros((8, width), F32)
    grams = lax.fori_loop(0, slots, gram, (empty,) * (len(pairs) + len(cross)))
    n_inner = 2 * krylov + 1
    part[...] = jnp.zeros(part.shape, F32)
    for n, x in enumerate(grams):
        part[n_inner + n : n_inner + n + 1, :] = fold(x)

    @pl.when(has_prev)
    def _():
        to_next.wait_recv()
        for c in range(2):
            img[c, 0] = img[c, 0] + (flw[0] * low[c, 0] + flw[1] * low[c, 1])
            img[c, 1] = img[c, 1] + flw[0] * low[c, 1]

    @pl.when(has_next)
    def _():
        to_prev.wait_recv()
        for c in range(2):
            one_up = jnp.where(upto < modes, up[c, 0], 0.0)
            two_up = jnp.where(upto + 1 < modes, up[c, 1], 0.0)
            on_last = flw[2] * one_up + flw[3] * two_up
            on_second = flw[3] * one_up
            for s in range(slots):
                term = jnp.where(s == count - 1, on_last, jnp.where(s == count - 2, on_second, 0.0))
                img[c, s] = img[c, s] + term

    inner = []
    for c in range(2):
        xh, xl = split(img[c].reshape(rows, width))
        y = mm(dh[1], xh) + mm(dl[1], xh) + mm(dh[1], xl)
        ends = split(y[rows : rows + 2 * slots])
        both = mmt(ends[0], rh[1]) + mmt(ends[1], rh[1]) + mmt(ends[0], rl[1])
        trs[mer, 0, c] = both[0:slots]
        trs[mer, 1, c] = both[slots : 2 * slots]
        inner.append(y[0:rows])

    def trace(i, slot, to):
        return pltpu.make_async_remote_copy(
            src_ref=trs.at[slot], dst_ref=trs.at[slot], send_sem=tr_send.at[i], recv_sem=tr_recv.at[i],
            device_id=at_mer(to), device_id_type=mesh_id,
        )

    for i in range(1, n_mer):
        trace(i, mer, lax.rem(mer + i, n_mer)).start()
    for c in range(2):
        yh, yl = split(inner[c])
        loc[c] = (mmt(yh, rh[1]) + mmt(yl, rh[1]) + mmt(yh, rl[1])).reshape(slots, points, width)
    for i in range(1, n_mer):
        trace(i, lax.rem(mer + n_mer - i, n_mer), mer).wait_recv()

    count_j = n_mer - 1
    inverse = np.linalg.inv(schur_diag * np.eye(count_j) - np.eye(count_j, k=1) - np.eye(count_j, k=-1))
    inverse = np.pad(inverse, ((1, 1), (0, 0)))
    jumps = [[trs[j, 0, c] - trs[j + 1, 1, c] for c in range(2)] for j in range(count_j)]

    def weight(side, j):
        value = jnp.float32(0.0)
        for b in range(n_mer):
            value = jnp.where(mer == b, jnp.float32(inverse[b + side, j]), value)
        return value

    sides = []
    for side in range(2):
        weights = [weight(side, j) for j in range(count_j)]
        sides.append([mask * sum(w * jump[c] for w, jump in zip(weights, jumps)) for c in range(2)])

    accs = [empty] * n_inner
    height = lax.broadcasted_iota(jnp.int32, (8, width), 0)
    for s in range(slots):
        live = s < count
        for t in range(tiles):
            z = slice(t * 8, (t + 1) * 8)
            position = (height + t * 8).astype(F32) / (points - 1)
            w = []
            for c in range(2):
                x = loc[c, s, z, :] + (1.0 - position) * sides[0][c][s : s + 1] - position * sides[1][c][s : s + 1]
                x = jnp.where(live, x, 0.0)
                loc[c, s, z, :] = x
                w.append(x)
            for j in range(krylov):
                src = cur if j == krylov - 1 else bas.at[j]
                re, im = src[0, s, z, :], src[1, s, z, :]
                accs[j] = accs[j] + (re * w[0] + im * w[1])
                accs[krylov + j] = accs[krylov + j] + (re * w[1] - im * w[0])
            accs[2 * krylov] = accs[2 * krylov] + (w[0] * w[0] + w[1] * w[1])
        pltpu.make_async_copy(loc.at[:, s], w_out.at[:, s], w_sem.at[s]).start()
    for n, x in enumerate(accs):
        part[n : n + 1, :] = fold(x)

    def share(buffer, sends, recvs, i, slot, device):
        return pltpu.make_async_remote_copy(
            src_ref=buffer.at[slot], dst_ref=buffer.at[slot], send_sem=sends.at[i], recv_sem=recvs.at[i],
            device_id=device, device_id_type=mesh_id,
        )

    red_mer[mer] = to_row(jnp.sum(part[...], axis=1, keepdims=True))
    for i in range(1, n_mer):
        share(red_mer, ra_send, ra_recv, i, mer, at_mer(lax.rem(mer + i, n_mer))).start()
    for i in range(1, n_mer):
        share(red_mer, ra_send, ra_recv, i, lax.rem(mer + n_mer - i, n_mer), at_mer(mer)).wait_recv()
    total = red_mer[0]
    for i in range(1, n_mer):
        total = total + red_mer[i]
    red_mode[mode] = total
    for i in range(1, n_mode):
        share(red_mode, rb_send, rb_recv, i, mode, at_mode(lax.rem(mode + i, n_mode))).start()
    for i in range(1, n_mode):
        share(red_mode, rb_send, rb_recv, i, lax.rem(mode + n_mode - i, n_mode), at_mode(mode)).wait_recv()
    total = red_mode[0]
    for i in range(1, n_mode):
        total = total + red_mode[i]
    lane = lax.broadcasted_iota(jnp.int32, (1, 128), 1)
    stats[...] = jnp.where(lane == 127, count.astype(F32), total)
    for s in range(slots):
        pltpu.make_async_copy(loc.at[:, s], w_out.at[:, s], w_sem.at[s]).wait()

    for there, copy in ((has_next, to_next), (has_prev, to_prev), (has_right, to_right), (has_left, to_left)):

        @pl.when(there)
        def _(copy=copy):
            copy.wait_send()

    for i in range(1, n_mer):
        trace(i, mer, lax.rem(mer + i, n_mer)).wait_send()
        share(red_mer, ra_send, ra_recv, i, mer, at_mer(lax.rem(mer + i, n_mer))).wait_send()
    for i in range(1, n_mode):
        share(red_mode, rb_send, rb_recv, i, mode, at_mode(lax.rem(mode + i, n_mode))).wait_send()


def body(n_mode, n_mer, mode_cost, iface_index, basis, radial, axial, flow_coupling, swirl, shift):
    krylov, _, slots, points, width = basis.shape
    modes = mode_cost.shape[0]
    rows = slots * points
    sums = 2 * krylov + 1 + krylov * krylov
    sums = (sums + 7) // 8 * 8
    field = (2, slots, points, width)
    pair = (2, 2, points, width)
    ends = (2, slots, width)
    smem = pl.BlockSpec(memory_space=pltpu.SMEM)
    hbm = pl.BlockSpec(memory_space=pl.ANY)
    vmem = pl.BlockSpec(memory_space=pltpu.VMEM)
    dma = pltpu.SemaphoreType.DMA
    w, stats = pl.pallas_call(
        functools.partial(kernel, n_mode, n_mer, modes),
        out_shape=[jax.ShapeDtypeStruct(field, F32), jax.ShapeDtypeStruct((1, 128), F32)],
        in_specs=[smem, smem] + [hbm] * 6,
        out_specs=[hbm, vmem],
        scratch_shapes=[
            pltpu.VMEM(field, F32),
            pltpu.VMEM((krylov - 1,) + field, F32),
            pltpu.VMEM(radial.shape, F32),
            pltpu.VMEM(axial.shape, F32),
            pltpu.VMEM(flow_coupling.shape, F32),
            pltpu.VMEM(swirl.shape, F32),
            pltpu.VMEM((1, iface_index.shape[0]), jnp.int32),
            pltpu.VMEM(pair, F32),
            pltpu.VMEM(pair, F32),
            pltpu.VMEM(pair, F32),
            pltpu.VMEM(ends, F32),
            pltpu.VMEM(ends, F32),
            pltpu.VMEM(ends, F32),
            pltpu.VMEM(ends, F32),
            pltpu.VMEM(radial.shape, BF16),
            pltpu.VMEM(radial.shape, BF16),
            pltpu.VMEM((2, rows + 2 * slots, rows), BF16),
            pltpu.VMEM((2, rows + 2 * slots, rows), BF16),
            pltpu.VMEM(field, F32),
            pltpu.VMEM(field, F32),
            pltpu.VMEM((n_mer, 2) + ends, F32),
            pltpu.VMEM((sums, 128), F32),
            pltpu.VMEM((n_mer, 1, 128), F32),
            pltpu.VMEM((n_mode, 1, 128), F32),
            dma((7,)),
            dma((slots,)),
            dma((4,)),
            dma((4,)),
            dma((n_mer,)),
            dma((n_mer,)),
            dma((n_mer,)),
            dma((n_mer,)),
            dma((n_mode,)),
            dma((n_mode,)),
        ],
        compiler_params=pltpu.CompilerParams(
            collective_id=0, has_side_effects=True, vmem_limit_bytes=60 * 1024 * 1024
        ),
    )(mode_cost, shift, iface_index[None, :], basis, radial, axial, flow_coupling, swirl)
    new_vector, coeffs, norm = pl.pallas_call(
        functools.partial(finish, float(modes * points * n_mer * width)),
        out_shape=[
            jax.ShapeDtypeStruct(field, F32),
            jax.ShapeDtypeStruct((2, krylov), F32),
            jax.ShapeDtypeStruct((1, 1), F32),
        ],
        in_specs=[hbm, hbm, vmem],
        out_specs=[hbm, vmem, vmem],
        scratch_shapes=[
            pltpu.VMEM(basis.shape, F32),
            pltpu.VMEM(field, F32),
            pltpu.VMEM(field, F32),
            dma((2,)),
            dma((2,)),
            dma((2,)),
        ],
        compiler_params=pltpu.CompilerParams(vmem_limit_bytes=60 * 1024 * 1024),
    )(basis, w, stats)
    return new_vector, coeffs, norm.reshape(())


def solution(mesh):
    in_specs = (
        P(),
        P(),
        P(None, None, "mode", "mer", None),
        P(),
        P(None, "mer", None),
        P(None, "mer", None),
        P("mer", None),
        P(),
    )
    out_specs = (P(None, "mode", "mer", None), P(), P())
    program = functools.partial(body, mesh.shape["mode"], mesh.shape["mer"])
    return jax.shard_map(program, mesh=mesh, in_specs=in_specs, out_specs=out_specs, check_vma=False)
```

```python
import functools

import jax
import jax.numpy as jnp
import numpy as np
from jax import lax
from jax.experimental import pallas as pl
from jax.experimental.pallas import tpu as pltpu
from jax.sharding import PartitionSpec as P

QUOTA = 840

penalty = 1.0
schur_diag = 2.2
epsilon = 1e-06

F32 = jnp.float32
BF16 = jnp.bfloat16


def split(x):
    hi = x.astype(BF16)
    return hi, (x - hi.astype(F32)).astype(BF16)


def mm(a, b):
    return lax.dot_general(a, b, (((1,), (0,)), ((), ())), preferred_element_type=F32)


def mmt(a, b):
    return lax.dot_general(a, b, (((1,), (1,)), ((), ())), preferred_element_type=F32)


def diagonal(size):
    row = lax.broadcasted_iota(jnp.int32, (size, 128), 0)
    return row == lax.broadcasted_iota(jnp.int32, (size, 128), 1)


def to_row(column):
    return jnp.sum(jnp.where(diagonal(column.shape[0]), column, 0.0), axis=0, keepdims=True)


def to_column(row, size):
    return jnp.sum(jnp.where(diagonal(size), row, 0.0), axis=1, keepdims=True)


def finish(dof, basis, w_in, stats, out, coef, norm, bas, w, fresh, in_sem, w_sem, out_sem):
    krylov, _, slots, points, width = basis.shape
    tiles = points // 8
    pairs = [(i, j) for i in range(krylov) for j in range(i, krylov)]
    cross = [(i, j) for i in range(krylov) for j in range(i + 1, krylov)]
    n_inner = 2 * krylov + 1
    sums = n_inner + len(pairs) + len(cross)
    ins, outs = [], []
    for n in range(slots):
        at = pl.ds(n, 1)
        ins.append(pltpu.make_async_copy(basis.at[:, :, at], bas.at[:, :, at], in_sem.at[n]))
        ins.append(pltpu.make_async_copy(w_in.at[:, at], w.at[:, at], w_sem.at[n]))
        outs.append(pltpu.make_async_copy(fresh.at[:, at], out.at[:, at], out_sem.at[n]))
    for copy in ins:
        copy.start()
    count = stats[:, 127:128]
    total = to_column(stats[...], (sums + 7) // 8 * 8) / dof
    one = [total[n : n + 1, :] for n in range(sums)]
    c_re, c_im = one[0:krylov], one[krylov : 2 * krylov]
    square = one[2 * krylov]
    for j in range(krylov):
        square = square - 2.0 * (c_re[j] * c_re[j] + c_im[j] * c_im[j])
    for n, (i, j) in enumerate(pairs):
        both = c_re[i] * c_re[j] + c_im[i] * c_im[j]
        square = square + (1.0 if i == j else 2.0) * both * one[n_inner + n]
    for n, (i, j) in enumerate(cross):
        both = c_re[i] * c_im[j] - c_im[i] * c_re[j]
        square = square - 2.0 * both * one[n_inner + len(pairs) + n]
    size = jnp.sqrt(jnp.maximum(square, 0.0) + epsilon)
    norm[...] = size
    lane = lax.broadcasted_iota(jnp.int32, coef.shape, 1)
    side = lax.broadcasted_iota(jnp.int32, coef.shape, 0)
    table = jnp.zeros(coef.shape, F32)
    for j in range(krylov):
        table = jnp.where(lane == j, jnp.where(side == 0, c_re[j], c_im[j]), table)
    coef[...] = table

    scale = 1.0 / size
    scaled_re = [jnp.broadcast_to(x * scale, (8, width)) for x in c_re]
    scaled_im = [jnp.broadcast_to(x * scale, (8, width)) for x in c_im]
    scale = jnp.broadcast_to(scale, (8, width))
    live_to = jnp.broadcast_to(count, (8, width))
    for s in range(slots):
        ins[2 * s].wait()
        ins[2 * s + 1].wait()
        live = live_to > s
        for t in range(tiles):
            z = slice(t * 8, (t + 1) * 8)
            new_re = w[0, s, z, :] * scale
            new_im = w[1, s, z, :] * scale
            for j in range(krylov):
                re, im = bas[j, 0, s, z, :], bas[j, 1, s, z, :]
                new_re = new_re - (scaled_re[j] * re - scaled_im[j] * im)
                new_im = new_im - (scaled_re[j] * im + scaled_im[j] * re)
            fresh[0, s, z, :] = jnp.where(live, new_re, 0.0)
            fresh[1, s, z, :] = jnp.where(live, new_im, 0.0)
        outs[s].start()
    for copy in outs:
        copy.wait()


def kernel(
    n_mode, n_mer, modes,
    cost, shift, iface, basis, radial, axial, flow, swirl,
    w_out, stats,
    cur, bas, rad, axl, flw, swl, ifc,
    stage, low, up, first, last, mlo, mhi,
    rh, rl, dh, dl, img, loc, trs, part, red_mer, red_mode,
    local_sem, w_sem, halo_send, halo_recv, tr_send, tr_recv, ra_send, ra_recv, rb_send, rb_recv,
):
    krylov, _, slots, points, width = basis.shape
    rows = slots * points
    tiles = points // 8
    mode = lax.axis_index("mode")
    mer = lax.axis_index("mer")

    def at_mode(i):
        return {"mode": i}

    def at_mer(i):
        return {"mer": i}

    mesh_id = pl.DeviceIdType.MESH
    barrier = pltpu.get_barrier_semaphore()
    for i in range(1, n_mer):
        pl.semaphore_signal(barrier, inc=1, device_id=at_mer(lax.rem(mer + i, n_mer)), device_id_type=mesh_id)
    for i in range(1, n_mode):
        pl.semaphore_signal(barrier, inc=1, device_id=at_mode(lax.rem(mode + i, n_mode)), device_id_type=mesh_id)

    loads = [
        pltpu.make_async_copy(basis.at[krylov - 1], cur, local_sem.at[0]),
        pltpu.make_async_copy(axial, axl, local_sem.at[1]),
        pltpu.make_async_copy(iface, ifc, local_sem.at[2]),
        pltpu.make_async_copy(radial, rad, local_sem.at[3]),
        pltpu.make_async_copy(flow, flw, local_sem.at[4]),
        pltpu.make_async_copy(swirl, swl, local_sem.at[5]),
        pltpu.make_async_copy(basis.at[0 : krylov - 1], bas, local_sem.at[6]),
    ]
    loads[0].start()

    least = mode * QUOTA

    def layout(k, carry):
        prefix, start, upto = carry
        start = start + (prefix < least).astype(jnp.int32)
        upto = upto + (prefix < least + QUOTA).astype(jnp.int32)
        return prefix + cost[k], start, upto

    zero = jnp.int32(0)
    _, start, upto = lax.fori_loop(0, modes, layout, (zero, zero, zero), unroll=8)
    count = upto - start
    ending = jnp.clip(count, 2, slots) - 2

    loads[0].wait()
    for c in range(2):
        for i in range(2):
            stage[c, i] = cur[c, ending + i]

    def halo(which, src, dst, device):
        return pltpu.make_async_remote_copy(
            src_ref=src, dst_ref=dst, send_sem=halo_send.at[which], recv_sem=halo_recv.at[which],
            device_id=device, device_id_type=mesh_id,
        )

    to_next = halo(0, stage, low, at_mode(lax.rem(mode + 1, n_mode)))
    to_prev = halo(1, cur.at[:, 0:2], up, at_mode(lax.rem(mode + n_mode - 1, n_mode)))
    to_right = halo(2, last, mlo, at_mer(lax.rem(mer + 1, n_mer)))
    to_left = halo(3, first, mhi, at_mer(lax.rem(mer + n_mer - 1, n_mer)))
    has_next, has_prev = mode < n_mode - 1, mode > 0
    has_right, has_left = mer < n_mer - 1, mer > 0
    pl.semaphore_wait(barrier, n_mer - 1 + n_mode - 1)
    for there, copy in ((has_next, to_next), (has_prev, to_prev)):

        @pl.when(there)
        def _(copy=copy):
            copy.start()

    for load in loads[1:]:
        load.start()
    for c in range(2):
        for s in range(slots):
            first[c, s : s + 1, :] = cur[c, s, 0:1, :]
            last[c, s : s + 1, :] = cur[c, s, points - 1 : points, :]
    for there, copy in ((has_right, to_right), (has_left, to_left)):

        @pl.when(there)
        def _(copy=copy):
            copy.start()

    loads[1].wait()
    col = lax.broadcasted_iota(jnp.int32, (points, width), 1)
    row = lax.broadcasted_iota(jnp.int32, (points, width), 0)
    spread = col == row
    for s in range(1, slots):
        spread = jnp.logical_or(spread, col == row + s * points)
    spread = jnp.where(spread, 1.0, 0.0).astype(BF16)
    col8 = lax.broadcasted_iota(jnp.int32, (slots, width), 1)
    base8 = lax.broadcasted_iota(jnp.int32, (slots, width), 0) * points
    mine8 = jnp.logical_and(col8 >= base8, col8 < base8 + points)
    for k in range(2):
        for part_of, to in zip(split(axl[k]), (dh, dl)):
            wide = mm(part_of, spread)
            for s in range(slots):
                block = jnp.logical_and(col >= s * points, col < (s + 1) * points)
                to[k, s * points : (s + 1) * points, :] = jnp.where(block, wide, 0.0).astype(BF16)
            if k == 1:
                top = jnp.where(mine8, jnp.broadcast_to(wide[points - 1 : points], (slots, width)), 0.0)
                bottom = jnp.where(mine8, jnp.broadcast_to(wide[0:1], (slots, width)), 0.0)
                to[k, rows : rows + 2 * slots, :] = jnp.concatenate([top, bottom], axis=0).astype(BF16)

    loads[2].wait()
    places = lax.broadcasted_iota(jnp.int32, (width, ifc.shape[1]), 0)
    chosen = jnp.where(places == ifc[...], 1.0, 0.0).astype(BF16)
    mask = mmt(jnp.ones((8, ifc.shape[1]), BF16), chosen)

    loads[3].wait()
    for k in range(2):
        rh[k], rl[k] = split(rad[k])
    for c in range(2):
        xh, xl = split(cur[c].reshape(rows, width))
        total = mmt(xh, rh[0]) + mmt(xl, rh[0]) + mmt(xh, rl[0])
        total = total + mm(dh[0, 0:rows], xh) + mm(dl[0, 0:rows], xh) + mm(dh[0, 0:rows], xl)
        img[c] = total.reshape(slots, points, width)

    loads[4].wait()
    loads[5].wait()

    @pl.when(has_left)
    def _():
        to_right.wait_recv()

    @pl.when(jnp.logical_not(has_left))
    def _():
        mlo[...] = jnp.zeros(mlo.shape, F32)

    @pl.when(has_right)
    def _():
        to_left.wait_recv()

    @pl.when(jnp.logical_not(has_right))
    def _():
        mhi[...] = jnp.zeros(mhi.shape, F32)

    sig_re, sig_im = shift[0], shift[1]
    sub8 = lax.broadcasted_iota(jnp.int32, (8, width), 0)
    offsets = (-2, -1, 1, 2)
    for s in range(slots):
        wave = (start + s).astype(F32) / modes
        for t in range(tiles):
            z = slice(t * 8, (t + 1) * 8)
            spin = sig_im - wave * swl[z, :]
            x = (cur[0, s, z, :], cur[1, s, z, :])
            for c in range(2):
                acc = img[c, s, z, :]
                for i, d in enumerate(offsets):
                    if 0 <= s + d < slots:
                        other = cur[c, s + d, z, :]
                        if d > 0:
                            other = jnp.where(s + d < count, other, 0.0)
                        acc = acc + flw[i, z, :] * other
                turn = spin * x[1] if c == 0 else -(spin * x[0])
                acc = acc - sig_re * x[c] + turn
                if t == 0:
                    acc = acc + jnp.where(sub8 == 0, penalty * mlo[c, s : s + 1, :], 0.0)
                if t == tiles - 1:
                    acc = acc + jnp.where(sub8 == 7, penalty * mhi[c, s : s + 1, :], 0.0)
                img[c, s, z, :] = acc

    loads[6].wait()
    pairs = [(i, j) for i in range(krylov) for j in range(i, krylov)]
    cross = [(i, j) for i in range(krylov) for j in range(i + 1, krylov)]

    def fold(x):
        half = x[:, 0:128]
        for at in range(128, width, 128):
            half = half + x[:, at : at + 128]
        return jnp.sum(half, axis=0, keepdims=True)

    def gram(s, carry):
        carry = list(carry)
        live = s < count
        for t in range(tiles):
            z = pl.ds(t * 8, 8)
            q = [[bas[j, c, s, z, :] for c in range(2)] for j in range(krylov - 1)]
            q.append([cur[c, s, z, :] for c in range(2)])
            q = [[jnp.where(live, x, 0.0) for x in both] for both in q]
            for n, (i, j) in enumerate(pairs):
                carry[n] = carry[n] + (q[i][0] * q[j][0] + q[i][1] * q[j][1])
            for n, (i, j) in enumerate(cross):
                n += len(pairs)
                carry[n] = carry[n] + (q[i][0] * q[j][1] - q[i][1] * q[j][0])
        return tuple(carry)

    empty = jnp.zeros((8, width), F32)
    grams = lax.fori_loop(0, slots, gram, (empty,) * (len(pairs) + len(cross)))
    n_inner = 2 * krylov + 1
    part[...] = jnp.zeros(part.shape, F32)
    for n, x in enumerate(grams):
        part[n_inner + n : n_inner + n + 1, :] = fold(x)

    @pl.when(has_prev)
    def _():
        to_next.wait_recv()
        for c in range(2):
            img[c, 0] = img[c, 0] + (flw[0] * low[c, 0] + flw[1] * low[c, 1])
            img[c, 1] = img[c, 1] + flw[0] * low[c, 1]

    @pl.when(has_next)
    def _():
        to_prev.wait_recv()
        for c in range(2):
            one_up = jnp.where(upto < modes, up[c, 0], 0.0)
            two_up = jnp.where(upto + 1 < modes, up[c, 1], 0.0)
            on_last = flw[2] * one_up + flw[3] * two_up
            on_second = flw[3] * one_up
            for s in range(slots):
                term = jnp.where(s == count - 1, on_last, jnp.where(s == count - 2, on_second, 0.0))
                img[c, s] = img[c, s] + term

    inner = []
    for c in range(2):
        xh, xl = split(img[c].reshape(rows, width))
        y = mm(dh[1], xh) + mm(dl[1], xh) + mm(dh[1], xl)
        ends = split(y[rows : rows + 2 * slots])
        both = mmt(ends[0], rh[1]) + mmt(ends[1], rh[1]) + mmt(ends[0], rl[1])
        trs[mer, 0, c] = both[0:slots]
        trs[mer, 1, c] = both[slots : 2 * slots]
        inner.append(y[0:rows])

    def trace(i, slot, to):
        return pltpu.make_async_remote_copy(
            src_ref=trs.at[slot], dst_ref=trs.at[slot], send_sem=tr_send.at[i], recv_sem=tr_recv.at[i],
            device_id=at_mer(to), device_id_type=mesh_id,
        )

    for i in range(1, n_mer):
        trace(i, mer, lax.rem(mer + i, n_mer)).start()
    for c in range(2):
        yh, yl = split(inner[c])
        loc[c] = (mmt(yh, rh[1]) + mmt(yl, rh[1]) + mmt(yh, rl[1])).reshape(slots, points, width)
    for i in range(1, n_mer):
        trace(i, lax.rem(mer + n_mer - i, n_mer), mer).wait_recv()

    count_j = n_mer - 1
    inverse = np.linalg.inv(schur_diag * np.eye(count_j) - np.eye(count_j, k=1) - np.eye(count_j, k=-1))
    inverse = np.pad(inverse, ((1, 1), (0, 0)))
    jumps = [[trs[j, 0, c] - trs[j + 1, 1, c] for c in range(2)] for j in range(count_j)]

    def weight(side, j):
        value = jnp.float32(0.0)
        for b in range(n_mer):
            value = jnp.where(mer == b, jnp.float32(inverse[b + side, j]), value)
        return value

    sides = []
    for side in range(2):
        weights = [weight(side, j) for j in range(count_j)]
        sides.append([mask * sum(w * jump[c] for w, jump in zip(weights, jumps)) for c in range(2)])

    accs = [empty] * n_inner
    height = lax.broadcasted_iota(jnp.int32, (8, width), 0)
    for s in range(slots):
        live = s < count
        for t in range(tiles):
            z = slice(t * 8, (t + 1) * 8)
            position = (height + t * 8).astype(F32) / (points - 1)
            w = []
            for c in range(2):
                x = loc[c, s, z, :] + (1.0 - position) * sides[0][c][s : s + 1] - position * sides[1][c][s : s + 1]
                x = jnp.where(live, x, 0.0)
                loc[c, s, z, :] = x
                w.append(x)
            for j in range(krylov):
                src = cur if j == krylov - 1 else bas.at[j]
                re, im = src[0, s, z, :], src[1, s, z, :]
                accs[j] = accs[j] + (re * w[0] + im * w[1])
                accs[krylov + j] = accs[krylov + j] + (re * w[1] - im * w[0])
            accs[2 * krylov] = accs[2 * krylov] + (w[0] * w[0] + w[1] * w[1])
        pltpu.make_async_copy(loc.at[:, s], w_out.at[:, s], w_sem.at[s]).start()
    for n, x in enumerate(accs):
        part[n : n + 1, :] = fold(x)

    def share(buffer, sends, recvs, i, slot, device):
        return pltpu.make_async_remote_copy(
            src_ref=buffer.at[slot], dst_ref=buffer.at[slot], send_sem=sends.at[i], recv_sem=recvs.at[i],
            device_id=device, device_id_type=mesh_id,
        )

    red_mer[mer] = to_row(jnp.sum(part[...], axis=1, keepdims=True))
    for i in range(1, n_mer):
        share(red_mer, ra_send, ra_recv, i, mer, at_mer(lax.rem(mer + i, n_mer))).start()
    for i in range(1, n_mer):
        share(red_mer, ra_send, ra_recv, i, lax.rem(mer + n_mer - i, n_mer), at_mer(mer)).wait_recv()
    total = red_mer[0]
    for i in range(1, n_mer):
        total = total + red_mer[i]
    red_mode[mode] = total
    for i in range(1, n_mode):
        share(red_mode, rb_send, rb_recv, i, mode, at_mode(lax.rem(mode + i, n_mode))).start()
    for i in range(1, n_mode):
        share(red_mode, rb_send, rb_recv, i, lax.rem(mode + n_mode - i, n_mode), at_mode(mode)).wait_recv()
    total = red_mode[0]
    for i in range(1, n_mode):
        total = total + red_mode[i]
    lane = lax.broadcasted_iota(jnp.int32, (1, 128), 1)
    stats[...] = jnp.where(lane == 127, count.astype(F32), total)
    for s in range(slots):
        pltpu.make_async_copy(loc.at[:, s], w_out.at[:, s], w_sem.at[s]).wait()

    for there, copy in ((has_next, to_next), (has_prev, to_prev), (has_right, to_right), (has_left, to_left)):

        @pl.when(there)
        def _(copy=copy):
            copy.wait_send()

    for i in range(1, n_mer):
        trace(i, mer, lax.rem(mer + i, n_mer)).wait_send()
        share(red_mer, ra_send, ra_recv, i, mer, at_mer(lax.rem(mer + i, n_mer))).wait_send()
    for i in range(1, n_mode):
        share(red_mode, rb_send, rb_recv, i, mode, at_mode(lax.rem(mode + i, n_mode))).wait_send()


def body(n_mode, n_mer, mode_cost, iface_index, basis, radial, axial, flow_coupling, swirl, shift):
    krylov, _, slots, points, width = basis.shape
    modes = mode_cost.shape[0]
    rows = slots * points
    sums = 2 * krylov + 1 + krylov * krylov
    sums = (sums + 7) // 8 * 8
    field = (2, slots, points, width)
    pair = (2, 2, points, width)
    ends = (2, slots, width)
    smem = pl.BlockSpec(memory_space=pltpu.SMEM)
    hbm = pl.BlockSpec(memory_space=pl.ANY)
    vmem = pl.BlockSpec(memory_space=pltpu.VMEM)
    dma = pltpu.SemaphoreType.DMA
    w, stats = pl.pallas_call(
        functools.partial(kernel, n_mode, n_mer, modes),
        out_shape=[jax.ShapeDtypeStruct(field, F32), jax.ShapeDtypeStruct((1, 128), F32)],
        in_specs=[smem, smem] + [hbm] * 6,
        out_specs=[hbm, vmem],
        scratch_shapes=[
            pltpu.VMEM(field, F32),
            pltpu.VMEM((krylov - 1,) + field, F32),
            pltpu.VMEM(radial.shape, F32),
            pltpu.VMEM(axial.shape, F32),
            pltpu.VMEM(flow_coupling.shape, F32),
            pltpu.VMEM(swirl.shape, F32),
            pltpu.VMEM((1, iface_index.shape[0]), jnp.int32),
            pltpu.VMEM(pair, F32),
            pltpu.VMEM(pair, F32),
            pltpu.VMEM(pair, F32),
            pltpu.VMEM(ends, F32),
            pltpu.VMEM(ends, F32),
            pltpu.VMEM(ends, F32),
            pltpu.VMEM(ends, F32),
            pltpu.VMEM(radial.shape, BF16),
            pltpu.VMEM(radial.shape, BF16),
            pltpu.VMEM((2, rows + 2 * slots, rows), BF16),
            pltpu.VMEM((2, rows + 2 * slots, rows), BF16),
            pltpu.VMEM(field, F32),
            pltpu.VMEM(field, F32),
            pltpu.VMEM((n_mer, 2) + ends, F32),
            pltpu.VMEM((sums, 128), F32),
            pltpu.VMEM((n_mer, 1, 128), F32),
            pltpu.VMEM((n_mode, 1, 128), F32),
            dma((7,)),
            dma((slots,)),
            dma((4,)),
            dma((4,)),
            dma((n_mer,)),
            dma((n_mer,)),
            dma((n_mer,)),
            dma((n_mer,)),
            dma((n_mode,)),
            dma((n_mode,)),
        ],
        compiler_params=pltpu.CompilerParams(
            collective_id=0, has_side_effects=True, vmem_limit_bytes=60 * 1024 * 1024
        ),
    )(mode_cost, shift, iface_index[None, :], basis, radial, axial, flow_coupling, swirl)
    new_vector, coeffs, norm = pl.pallas_call(
        functools.partial(finish, float(modes * points * n_mer * width)),
        out_shape=[
            jax.ShapeDtypeStruct(field, F32),
            jax.ShapeDtypeStruct((2, krylov), F32),
            jax.ShapeDtypeStruct((1, 1), F32),
        ],
        in_specs=[hbm, hbm, vmem],
        out_specs=[hbm, vmem, vmem],
        scratch_shapes=[
            pltpu.VMEM(basis.shape, F32),
            pltpu.VMEM(field, F32),
            pltpu.VMEM(field, F32),
            dma((slots,)),
            dma((slots,)),
            dma((slots,)),
        ],
        compiler_params=pltpu.CompilerParams(vmem_limit_bytes=60 * 1024 * 1024),
    )(basis, w, stats)
    return new_vector, coeffs, norm.reshape(())


def solution(mesh):
    in_specs = (
        P(),
        P(),
        P(None, None, "mode", "mer", None),
        P(),
        P(None, "mer", None),
        P(None, "mer", None),
        P("mer", None),
        P(),
    )
    out_specs = (P(None, "mode", "mer", None), P(), P())
    program = functools.partial(body, mesh.shape["mode"], mesh.shape["mer"])
    return jax.shard_map(program, mesh=mesh, in_specs=in_specs, out_specs=out_specs, check_vma=False)
```

```python
import functools

import jax
import jax.numpy as jnp
import numpy as np
from jax import lax
from jax.experimental import pallas as pl
from jax.experimental.pallas import tpu as pltpu
from jax.sharding import PartitionSpec as P

QUOTA = 840

penalty = 1.0
schur_diag = 2.2
epsilon = 1e-06

F32 = jnp.float32
BF16 = jnp.bfloat16


def split(x):
    hi = x.astype(BF16)
    return hi, (x - hi.astype(F32)).astype(BF16)


def mm(a, b):
    return lax.dot_general(a, b, (((1,), (0,)), ((), ())), preferred_element_type=F32)


def mmt(a, b):
    return lax.dot_general(a, b, (((1,), (1,)), ((), ())), preferred_element_type=F32)


def diagonal(size):
    row = lax.broadcasted_iota(jnp.int32, (size, 128), 0)
    return row == lax.broadcasted_iota(jnp.int32, (size, 128), 1)


def to_row(column):
    return jnp.sum(jnp.where(diagonal(column.shape[0]), column, 0.0), axis=0, keepdims=True)


def to_column(row, size):
    return jnp.sum(jnp.where(diagonal(size), row, 0.0), axis=1, keepdims=True)


def finish(dof, basis, w_in, stats, out, coef, norm, bas, w, fresh, in_sem, w_sem, out_sem):
    krylov, _, slots, points, width = basis.shape
    tiles = points // 8
    pairs = [(i, j) for i in range(krylov) for j in range(i, krylov)]
    cross = [(i, j) for i in range(krylov) for j in range(i + 1, krylov)]
    n_inner = 2 * krylov + 1
    sums = n_inner + len(pairs) + len(cross)
    ins, outs = [], []
    for n in range(slots):
        at = pl.ds(n, 1)
        ins.append(pltpu.make_async_copy(basis.at[:, :, at], bas.at[:, :, at], in_sem.at[n]))
        ins.append(pltpu.make_async_copy(w_in.at[:, at], w.at[:, at], w_sem.at[n]))
        outs.append(pltpu.make_async_copy(fresh.at[:, at], out.at[:, at], out_sem.at[n]))
    for copy in ins:
        copy.start()
    count = stats[:, 127:128]
    total = to_column(stats[...], (sums + 7) // 8 * 8) / dof
    one = [total[n : n + 1, :] for n in range(sums)]
    c_re, c_im = one[0:krylov], one[krylov : 2 * krylov]
    square = one[2 * krylov]
    for j in range(krylov):
        square = square - 2.0 * (c_re[j] * c_re[j] + c_im[j] * c_im[j])
    for n, (i, j) in enumerate(pairs):
        both = c_re[i] * c_re[j] + c_im[i] * c_im[j]
        square = square + (1.0 if i == j else 2.0) * both * one[n_inner + n]
    for n, (i, j) in enumerate(cross):
        both = c_re[i] * c_im[j] - c_im[i] * c_re[j]
        square = square - 2.0 * both * one[n_inner + len(pairs) + n]
    size = jnp.sqrt(jnp.maximum(square, 0.0) + epsilon)
    norm[...] = size
    lane = lax.broadcasted_iota(jnp.int32, coef.shape, 1)
    side = lax.broadcasted_iota(jnp.int32, coef.shape, 0)
    table = jnp.zeros(coef.shape, F32)
    for j in range(krylov):
        table = jnp.where(lane == j, jnp.where(side == 0, c_re[j], c_im[j]), table)
    coef[...] = table

    scale = 1.0 / size
    scaled_re = [jnp.broadcast_to(x * scale, (8, width)) for x in c_re]
    scaled_im = [jnp.broadcast_to(x * scale, (8, width)) for x in c_im]
    scale = jnp.broadcast_to(scale, (8, width))
    live_to = jnp.broadcast_to(count, (8, width))
    for s in range(slots):
        ins[2 * s].wait()
        ins[2 * s + 1].wait()
        live = live_to > s
        for t in range(tiles):
            z = slice(t * 8, (t + 1) * 8)
            new_re = w[0, s, z, :] * scale
            new_im = w[1, s, z, :] * scale
            for j in range(krylov):
                re, im = bas[j, 0, s, z, :], bas[j, 1, s, z, :]
                new_re = new_re - (scaled_re[j] * re - scaled_im[j] * im)
                new_im = new_im - (scaled_re[j] * im + scaled_im[j] * re)
            fresh[0, s, z, :] = jnp.where(live, new_re, 0.0)
            fresh[1, s, z, :] = jnp.where(live, new_im, 0.0)
        outs[s].start()
    for copy in outs:
        copy.wait()


def kernel(
    n_mode, n_mer, modes,
    cost, shift, iface, basis, radial, axial, flow, swirl,
    w_out, stats,
    cur, bas, rad, axl, flw, swl, ifc,
    stage, low, up, first, last, mlo, mhi,
    rh, rl, dh, dl, img, loc, trs, part, red_mer, red_mode,
    local_sem, w_sem, halo_send, halo_recv, tr_send, tr_recv, ra_send, ra_recv, rb_send, rb_recv,
):
    krylov, _, slots, points, width = basis.shape
    rows = slots * points
    tiles = points // 8
    mode = lax.axis_index("mode")
    mer = lax.axis_index("mer")

    def at_mode(i):
        return {"mode": i}

    def at_mer(i):
        return {"mer": i}

    mesh_id = pl.DeviceIdType.MESH
    barrier = pltpu.get_barrier_semaphore()
    for i in range(1, n_mer):
        pl.semaphore_signal(barrier, inc=1, device_id=at_mer(lax.rem(mer + i, n_mer)), device_id_type=mesh_id)
    for i in range(1, n_mode):
        pl.semaphore_signal(barrier, inc=1, device_id=at_mode(lax.rem(mode + i, n_mode)), device_id_type=mesh_id)

    loads = [
        pltpu.make_async_copy(basis.at[krylov - 1], cur, local_sem.at[0]),
        pltpu.make_async_copy(axial, axl, local_sem.at[1]),
        pltpu.make_async_copy(iface, ifc, local_sem.at[2]),
        pltpu.make_async_copy(radial, rad, local_sem.at[3]),
        pltpu.make_async_copy(flow, flw, local_sem.at[4]),
        pltpu.make_async_copy(swirl, swl, local_sem.at[5]),
        pltpu.make_async_copy(basis.at[0 : krylov - 1], bas, local_sem.at[6]),
    ]
    loads[0].start()

    least = mode * QUOTA

    def layout(k, carry):
        prefix, start, upto = carry
        start = start + (prefix < least).astype(jnp.int32)
        upto = upto + (prefix < least + QUOTA).astype(jnp.int32)
        return prefix + cost[k], start, upto

    zero = jnp.int32(0)
    _, start, upto = lax.fori_loop(0, modes, layout, (zero, zero, zero), unroll=8)
    count = upto - start
    ending = jnp.clip(count, 2, slots) - 2

    loads[0].wait()
    for c in range(2):
        for i in range(2):
            stage[c, i] = cur[c, ending + i]

    def halo(which, src, dst, device):
        return pltpu.make_async_remote_copy(
            src_ref=src, dst_ref=dst, send_sem=halo_send.at[which], recv_sem=halo_recv.at[which],
            device_id=device, device_id_type=mesh_id,
        )

    to_next = halo(0, stage, low, at_mode(lax.rem(mode + 1, n_mode)))
    to_prev = halo(1, cur.at[:, 0:2], up, at_mode(lax.rem(mode + n_mode - 1, n_mode)))
    to_right = halo(2, last, mlo, at_mer(lax.rem(mer + 1, n_mer)))
    to_left = halo(3, first, mhi, at_mer(lax.rem(mer + n_mer - 1, n_mer)))
    has_next, has_prev = mode < n_mode - 1, mode > 0
    has_right, has_left = mer < n_mer - 1, mer > 0
    pl.semaphore_wait(barrier, n_mer - 1 + n_mode - 1)
    for there, copy in ((has_next, to_next), (has_prev, to_prev)):

        @pl.when(there)
        def _(copy=copy):
            copy.start()

    for load in loads[1:]:
        load.start()
    for c in range(2):
        for s in range(slots):
            first[c, s : s + 1, :] = cur[c, s, 0:1, :]
            last[c, s : s + 1, :] = cur[c, s, points - 1 : points, :]
    for there, copy in ((has_right, to_right), (has_left, to_left)):

        @pl.when(there)
        def _(copy=copy):
            copy.start()

    loads[1].wait()
    col = lax.broadcasted_iota(jnp.int32, (points, width), 1)
    row = lax.broadcasted_iota(jnp.int32, (points, width), 0)
    spread = col == row
    for s in range(1, slots):
        spread = jnp.logical_or(spread, col == row + s * points)
    spread = jnp.where(spread, 1.0, 0.0).astype(BF16)
    col8 = lax.broadcasted_iota(jnp.int32, (slots, width), 1)
    base8 = lax.broadcasted_iota(jnp.int32, (slots, width), 0) * points
    mine8 = jnp.logical_and(col8 >= base8, col8 < base8 + points)
    for k in range(2):
        for part_of, to in zip(split(axl[k]), (dh, dl)):
            wide = mm(part_of, spread)
            for s in range(slots):
                block = jnp.logical_and(col >= s * points, col < (s + 1) * points)
                to[k, s * points : (s + 1) * points, :] = jnp.where(block, wide, 0.0).astype(BF16)
            if k == 1:
                top = jnp.where(mine8, jnp.broadcast_to(wide[points - 1 : points], (slots, width)), 0.0)
                bottom = jnp.where(mine8, jnp.broadcast_to(wide[0:1], (slots, width)), 0.0)
                to[k, rows : rows + 2 * slots, :] = jnp.concatenate([top, bottom], axis=0).astype(BF16)

    loads[2].wait()
    places = lax.broadcasted_iota(jnp.int32, (width, ifc.shape[1]), 0)
    chosen = jnp.where(places == ifc[...], 1.0, 0.0).astype(BF16)
    mask = mmt(jnp.ones((8, ifc.shape[1]), BF16), chosen)

    loads[3].wait()
    for k in range(2):
        rh[k], rl[k] = split(rad[k])
    for c in range(2):
        xh, xl = split(cur[c].reshape(rows, width))
        total = mmt(xh, rh[0]) + mmt(xl, rh[0]) + mmt(xh, rl[0])
        total = total + mm(dh[0, 0:rows], xh) + mm(dl[0, 0:rows], xh) + mm(dh[0, 0:rows], xl)
        img[c] = total.reshape(slots, points, width)

    loads[4].wait()
    loads[5].wait()

    @pl.when(has_left)
    def _():
        to_right.wait_recv()

    @pl.when(jnp.logical_not(has_left))
    def _():
        mlo[...] = jnp.zeros(mlo.shape, F32)

    @pl.when(has_right)
    def _():
        to_left.wait_recv()

    @pl.when(jnp.logical_not(has_right))
    def _():
        mhi[...] = jnp.zeros(mhi.shape, F32)

    sig_re, sig_im = shift[0], shift[1]
    sub8 = lax.broadcasted_iota(jnp.int32, (8, width), 0)
    offsets = (-2, -1, 1, 2)
    for s in range(slots):
        wave = (start + s).astype(F32) / modes
        for t in range(tiles):
            z = slice(t * 8, (t + 1) * 8)
            spin = sig_im - wave * swl[z, :]
            x = (cur[0, s, z, :], cur[1, s, z, :])
            for c in range(2):
                acc = img[c, s, z, :]
                for i, d in enumerate(offsets):
                    if 0 <= s + d < slots:
                        other = cur[c, s + d, z, :]
                        if d > 0:
                            other = jnp.where(s + d < count, other, 0.0)
                        acc = acc + flw[i, z, :] * other
                turn = spin * x[1] if c == 0 else -(spin * x[0])
                acc = acc - sig_re * x[c] + turn
                if t == 0:
                    acc = acc + jnp.where(sub8 == 0, penalty * mlo[c, s : s + 1, :], 0.0)
                if t == tiles - 1:
                    acc = acc + jnp.where(sub8 == 7, penalty * mhi[c, s : s + 1, :], 0.0)
                img[c, s, z, :] = acc

    @pl.when(has_prev)
    def _():
        to_next.wait_recv()
        for c in range(2):
            img[c, 0] = img[c, 0] + (flw[0] * low[c, 0] + flw[1] * low[c, 1])
            img[c, 1] = img[c, 1] + flw[0] * low[c, 1]

    @pl.when(has_next)
    def _():
        to_prev.wait_recv()
        for c in range(2):
            one_up = jnp.where(upto < modes, up[c, 0], 0.0)
            two_up = jnp.where(upto + 1 < modes, up[c, 1], 0.0)
            on_last = flw[2] * one_up + flw[3] * two_up
            on_second = flw[3] * one_up
            for s in range(slots):
                term = jnp.where(s == count - 1, on_last, jnp.where(s == count - 2, on_second, 0.0))
                img[c, s] = img[c, s] + term

    inner = []
    for c in range(2):
        xh, xl = split(img[c].reshape(rows, width))
        y = mm(dh[1], xh) + mm(dl[1], xh) + mm(dh[1], xl)
        ends = split(y[rows : rows + 2 * slots])
        both = mmt(ends[0], rh[1]) + mmt(ends[1], rh[1]) + mmt(ends[0], rl[1])
        trs[mer, 0, c] = both[0:slots]
        trs[mer, 1, c] = both[slots : 2 * slots]
        inner.append(y[0:rows])

    def trace(i, slot, to):
        return pltpu.make_async_remote_copy(
            src_ref=trs.at[slot], dst_ref=trs.at[slot], send_sem=tr_send.at[i], recv_sem=tr_recv.at[i],
            device_id=at_mer(to), device_id_type=mesh_id,
        )

    for i in range(1, n_mer):
        trace(i, mer, lax.rem(mer + i, n_mer)).start()
    for c in range(2):
        yh, yl = split(inner[c])
        loc[c] = (mmt(yh, rh[1]) + mmt(yl, rh[1]) + mmt(yh, rl[1])).reshape(slots, points, width)
    loads[6].wait()
    pairs = [(i, j) for i in range(krylov) for j in range(i, krylov)]
    cross = [(i, j) for i in range(krylov) for j in range(i + 1, krylov)]

    def fold(x):
        half = x[:, 0:128]
        for at in range(128, width, 128):
            half = half + x[:, at : at + 128]
        return jnp.sum(half, axis=0, keepdims=True)

    def gram(s, carry):
        carry = list(carry)
        live = s < count
        for t in range(tiles):
            z = pl.ds(t * 8, 8)
            q = [[bas[j, c, s, z, :] for c in range(2)] for j in range(krylov - 1)]
            q.append([cur[c, s, z, :] for c in range(2)])
            q = [[jnp.where(live, x, 0.0) for x in both] for both in q]
            for n, (i, j) in enumerate(pairs):
                carry[n] = carry[n] + (q[i][0] * q[j][0] + q[i][1] * q[j][1])
            for n, (i, j) in enumerate(cross):
                n += len(pairs)
                carry[n] = carry[n] + (q[i][0] * q[j][1] - q[i][1] * q[j][0])
        return tuple(carry)

    empty = jnp.zeros((8, width), F32)
    grams = lax.fori_loop(0, slots, gram, (empty,) * (len(pairs) + len(cross)))
    n_inner = 2 * krylov + 1
    part[...] = jnp.zeros(part.shape, F32)
    for n, x in enumerate(grams):
        part[n_inner + n : n_inner + n + 1, :] = fold(x)

    for i in range(1, n_mer):
        trace(i, lax.rem(mer + n_mer - i, n_mer), mer).wait_recv()

    count_j = n_mer - 1
    inverse = np.linalg.inv(schur_diag * np.eye(count_j) - np.eye(count_j, k=1) - np.eye(count_j, k=-1))
    inverse = np.pad(inverse, ((1, 1), (0, 0)))
    jumps = [[trs[j, 0, c] - trs[j + 1, 1, c] for c in range(2)] for j in range(count_j)]

    def weight(side, j):
        value = jnp.float32(0.0)
        for b in range(n_mer):
            value = jnp.where(mer == b, jnp.float32(inverse[b + side, j]), value)
        return value

    sides = []
    for side in range(2):
        weights = [weight(side, j) for j in range(count_j)]
        sides.append([mask * sum(w * jump[c] for w, jump in zip(weights, jumps)) for c in range(2)])

    accs = [empty] * n_inner
    height = lax.broadcasted_iota(jnp.int32, (8, width), 0)
    for s in range(slots):
        live = s < count
        for t in range(tiles):
            z = slice(t * 8, (t + 1) * 8)
            position = (height + t * 8).astype(F32) / (points - 1)
            w = []
            for c in range(2):
                x = loc[c, s, z, :] + (1.0 - position) * sides[0][c][s : s + 1] - position * sides[1][c][s : s + 1]
                x = jnp.where(live, x, 0.0)
                loc[c, s, z, :] = x
                w.append(x)
            for j in range(krylov):
                src = cur if j == krylov - 1 else bas.at[j]
                re, im = src[0, s, z, :], src[1, s, z, :]
                accs[j] = accs[j] + (re * w[0] + im * w[1])
                accs[krylov + j] = accs[krylov + j] + (re * w[1] - im * w[0])
            accs[2 * krylov] = accs[2 * krylov] + (w[0] * w[0] + w[1] * w[1])
        pltpu.make_async_copy(loc.at[:, s], w_out.at[:, s], w_sem.at[s]).start()
    for n, x in enumerate(accs):
        part[n : n + 1, :] = fold(x)

    def share(buffer, sends, recvs, i, slot, device):
        return pltpu.make_async_remote_copy(
            src_ref=buffer.at[slot], dst_ref=buffer.at[slot], send_sem=sends.at[i], recv_sem=recvs.at[i],
            device_id=device, device_id_type=mesh_id,
        )

    red_mer[mer] = to_row(jnp.sum(part[...], axis=1, keepdims=True))
    for i in range(1, n_mer):
        share(red_mer, ra_send, ra_recv, i, mer, at_mer(lax.rem(mer + i, n_mer))).start()
    for i in range(1, n_mer):
        share(red_mer, ra_send, ra_recv, i, lax.rem(mer + n_mer - i, n_mer), at_mer(mer)).wait_recv()
    total = red_mer[0]
    for i in range(1, n_mer):
        total = total + red_mer[i]
    red_mode[mode] = total
    for i in range(1, n_mode):
        share(red_mode, rb_send, rb_recv, i, mode, at_mode(lax.rem(mode + i, n_mode))).start()
    for i in range(1, n_mode):
        share(red_mode, rb_send, rb_recv, i, lax.rem(mode + n_mode - i, n_mode), at_mode(mode)).wait_recv()
    total = red_mode[0]
    for i in range(1, n_mode):
        total = total + red_mode[i]
    lane = lax.broadcasted_iota(jnp.int32, (1, 128), 1)
    stats[...] = jnp.where(lane == 127, count.astype(F32), total)
    for s in range(slots):
        pltpu.make_async_copy(loc.at[:, s], w_out.at[:, s], w_sem.at[s]).wait()

    for there, copy in ((has_next, to_next), (has_prev, to_prev), (has_right, to_right), (has_left, to_left)):

        @pl.when(there)
        def _(copy=copy):
            copy.wait_send()

    for i in range(1, n_mer):
        trace(i, mer, lax.rem(mer + i, n_mer)).wait_send()
        share(red_mer, ra_send, ra_recv, i, mer, at_mer(lax.rem(mer + i, n_mer))).wait_send()
    for i in range(1, n_mode):
        share(red_mode, rb_send, rb_recv, i, mode, at_mode(lax.rem(mode + i, n_mode))).wait_send()


def body(n_mode, n_mer, mode_cost, iface_index, basis, radial, axial, flow_coupling, swirl, shift):
    krylov, _, slots, points, width = basis.shape
    modes = mode_cost.shape[0]
    rows = slots * points
    sums = 2 * krylov + 1 + krylov * krylov
    sums = (sums + 7) // 8 * 8
    field = (2, slots, points, width)
    pair = (2, 2, points, width)
    ends = (2, slots, width)
    smem = pl.BlockSpec(memory_space=pltpu.SMEM)
    hbm = pl.BlockSpec(memory_space=pl.ANY)
    vmem = pl.BlockSpec(memory_space=pltpu.VMEM)
    dma = pltpu.SemaphoreType.DMA
    w, stats = pl.pallas_call(
        functools.partial(kernel, n_mode, n_mer, modes),
        out_shape=[jax.ShapeDtypeStruct(field, F32), jax.ShapeDtypeStruct((1, 128), F32)],
        in_specs=[smem, smem] + [hbm] * 6,
        out_specs=[hbm, vmem],
        scratch_shapes=[
            pltpu.VMEM(field, F32),
            pltpu.VMEM((krylov - 1,) + field, F32),
            pltpu.VMEM(radial.shape, F32),
            pltpu.VMEM(axial.shape, F32),
            pltpu.VMEM(flow_coupling.shape, F32),
            pltpu.VMEM(swirl.shape, F32),
            pltpu.VMEM((1, iface_index.shape[0]), jnp.int32),
            pltpu.VMEM(pair, F32),
            pltpu.VMEM(pair, F32),
            pltpu.VMEM(pair, F32),
            pltpu.VMEM(ends, F32),
            pltpu.VMEM(ends, F32),
            pltpu.VMEM(ends, F32),
            pltpu.VMEM(ends, F32),
            pltpu.VMEM(radial.shape, BF16),
            pltpu.VMEM(radial.shape, BF16),
            pltpu.VMEM((2, rows + 2 * slots, rows), BF16),
            pltpu.VMEM((2, rows + 2 * slots, rows), BF16),
            pltpu.VMEM(field, F32),
            pltpu.VMEM(field, F32),
            pltpu.VMEM((n_mer, 2) + ends, F32),
            pltpu.VMEM((sums, 128), F32),
            pltpu.VMEM((n_mer, 1, 128), F32),
            pltpu.VMEM((n_mode, 1, 128), F32),
            dma((7,)),
            dma((slots,)),
            dma((4,)),
            dma((4,)),
            dma((n_mer,)),
            dma((n_mer,)),
            dma((n_mer,)),
            dma((n_mer,)),
            dma((n_mode,)),
            dma((n_mode,)),
        ],
        compiler_params=pltpu.CompilerParams(
            collective_id=0, has_side_effects=True, vmem_limit_bytes=60 * 1024 * 1024
        ),
    )(mode_cost, shift, iface_index[None, :], basis, radial, axial, flow_coupling, swirl)
    new_vector, coeffs, norm = pl.pallas_call(
        functools.partial(finish, float(modes * points * n_mer * width)),
        out_shape=[
            jax.ShapeDtypeStruct(field, F32),
            jax.ShapeDtypeStruct((2, krylov), F32),
            jax.ShapeDtypeStruct((1, 1), F32),
        ],
        in_specs=[hbm, hbm, vmem],
        out_specs=[hbm, vmem, vmem],
        scratch_shapes=[
            pltpu.VMEM(basis.shape, F32),
            pltpu.VMEM(field, F32),
            pltpu.VMEM(field, F32),
            dma((slots,)),
            dma((slots,)),
            dma((slots,)),
        ],
        compiler_params=pltpu.CompilerParams(vmem_limit_bytes=60 * 1024 * 1024),
    )(basis, w, stats)
    return new_vector, coeffs, norm.reshape(())


def solution(mesh):
    in_specs = (
        P(),
        P(),
        P(None, None, "mode", "mer", None),
        P(),
        P(None, "mer", None),
        P(None, "mer", None),
        P("mer", None),
        P(),
    )
    out_specs = (P(None, "mode", "mer", None), P(), P())
    program = functools.partial(body, mesh.shape["mode"], mesh.shape["mer"])
    return jax.shard_map(program, mesh=mesh, in_specs=in_specs, out_specs=out_specs, check_vma=False)
```
